128 devices in a mesh: sec: 2 (over core), dev: 64 (over x, z, y).
Axes of the slice: x: 4, y: 4, z: 4, core: 2. Of those that a mesh axis runs over, the one named last changes fastest.
Arguments:
- hidden_in: bfloat16 [256, 7168], P(('sec', 'dev')), may hold values from -0.29882812 to 0.29882812
- queries: bfloat16 [256, 128, 576], P(('sec', 'dev')), may hold values from -40 to 40
- latent_cache: bfloat16 [256, 2048, 576], P(('sec', 'dev')), may hold values from -4.5 to 4.5
- cache_lengths: int32 [256], P(('sec', 'dev')), may hold values from 2 to 2048, as said below
- value_up: bfloat16 [128, 512, 128], P(('sec', 'dev')), may hold values from -0.25 to 0.25
- out_proj: bfloat16 [16384, 7168], P(('sec', 'dev')), may hold values from -0.046875 to 0.046875
- norm_gain: float32 [7168], replicated, may hold values from 0.5 to 1.5
- expert_ids: int32 [256, 8], P(('sec', 'dev')), may hold values from 0 to 15, all different within a row; in each aligned block of 2 rows (0 to 1, 2 to 3, ...) at most 2 rows name the same one
- route_weights: float32 [256, 8], P(('sec', 'dev')), may hold values from 0.1 to 0.5
- w_gate: bfloat16 [7168, 32768], P(None, ('sec', 'dev')), may hold values from -0.0625 to 0.0625
- w_up: bfloat16 [7168, 32768], P(None, ('sec', 'dev')), may hold values from -0.0625 to 0.0625
- w_down: bfloat16 [32768, 7168], P(('sec', 'dev')), may hold values from -0.125 to 0.125
Outputs:
- layer_out: bfloat16 [256, 7168], P(('sec', 'dev'))
The draws below stay inside these ranges and needn't reach their ends.
Inputs may be any that keep to these rules, and one draw needn't show every extreme that they name: `expert_ids`: each row names 8 different experts, and in the rows of one device no expert is named by more than 2 rows. `cache_lengths`: some row has exactly 2048 live positions.
All inputs are finite; a program needn't handle non-finite values.
Results may differ from the reference program's by a relative error of at most 0.022.
Values may be sent and summed in bfloat16 or wider, within the bound.
A program may use at most 128 MiB of HBM per device.

```python
import math
import jax
import jax.numpy as jnp
import numpy as np
from jax import lax

D = 7168
H = 128
LAT = 512
ROPE = 64
VH = 128
FF = 2048
TOP = 8
EXPERTS = 16
ROWS_DEV = 2
LEN = 2048
MOST = 2
ROWS = 256
N_SEC = 2
N_DEV = 64


def cache_base(key):
    return jnp.clip(jax.random.normal(key, (ROWS, LEN, LAT + ROPE), jnp.float32), -4.5, 4.5)


def draw_latent_cache(key, part):
    base = cache_base(key)
    return base.astype(jnp.bfloat16)


def draw_queries(key, part):
    key = jax.random.fold_in(key, 7)
    query = jnp.clip(jax.random.normal(key, (ROWS, H, LAT + ROPE), jnp.float32), -4.5, 4.5)
    return query.astype(jnp.bfloat16)


def draw_cache_lengths(key, part):
    key = jax.random.fold_in(key, 11)
    first, second, third = jax.random.split(key, 3)
    left = jax.random.randint(first, (ROWS,), 0, LEN - 1)
    right = jax.random.randint(second, (ROWS,), 0, LEN - 1)
    length = 2 + left * right // LEN
    length = jnp.minimum(length, LEN)
    chosen = jax.random.randint(third, (), 0, ROWS)
    length = jnp.where(jnp.arange(ROWS, dtype=jnp.int32) == chosen, LEN, length)
    return length.astype(jnp.int32)


def steps_of(rng, extent, cuts, least, largest):
    def one(position, blocks):
        heights = jax.random.uniform(jax.random.fold_in(jax.random.fold_in(rng, 6), position), (blocks,), jnp.float32, least / len(cuts), largest / len(cuts))
        return jnp.repeat(jnp.exp(heights), extent[position] // blocks).reshape((-1,) + (1,) * (len(extent) - position - 1))

    loudness = one(*cuts[0])
    for cut in cuts[1:]:
        loudness = loudness * one(*cut)
    return loudness


def shared_out(rng, own, number, rows, number_of, top, bound, skew):
    ranking = jax.random.permutation(rng, number_of)
    heavy_load, common = load_shares(number_of, rows * top, bound, skew, True), load_shares(number_of, rows * top, bound, skew, False)
    places = jnp.arange(number_of)

    def named(lengths, rotation):
        used = int((lengths > 0).sum())
        fixed = max(1, used // 4)
        passed = fixed + (places - fixed + rotation * (used - fixed)) % max(1, number_of - fixed)
        return jnp.zeros((number_of,), jnp.int32).at[ranking[jnp.where(places < fixed, places, passed)]].set(jnp.asarray(lengths, jnp.int32))

    lengths = jnp.where(number % 4 == 0, named(heavy_load, number // 4), named(common, number - number // 4 - 1))
    mixed = jax.random.permutation(jax.random.fold_in(own, 3), number_of)
    donor, sink = mixed[0:number_of // 2 * 2:2], mixed[1:number_of // 2 * 2:2]
    room = jnp.minimum(lengths[donor] - 1, bound - lengths[sink]) // 2
    room = jnp.where((donor == ranking[0]) | (sink == ranking[0]) | (lengths[sink] == 0), 0, jnp.maximum(room, 0))
    passed = jax.random.randint(jax.random.fold_in(own, 4), (number_of // 2,), 0, 1 << 20) % (room + 1)
    lengths = lengths.at[donor].add(-passed).at[sink].add(passed)
    items = jnp.searchsorted(jnp.cumsum(lengths), jnp.arange(rows * top), side="right").astype(jnp.int32)
    table = items.reshape(top, rows).T
    table = table[jax.random.permutation(jax.random.fold_in(own, 1), rows)]
    rotation = jax.random.randint(jax.random.fold_in(own, 2), (rows, 1), 0, top)
    return jnp.take_along_axis(table, (jnp.arange(top)[None, :] + rotation) % top, axis=1)


def load_shares(amount, total, reach, lean, full):
    weights = [(1 << 20) // math.isqrt(rank ** lean) + 1 for rank in range(1, amount + 1)]
    largest = reach if full else min(reach, max(-(-total // amount), total * weights[0] // sum(weights)))
    least = 1 if total - largest >= amount - 1 else 0
    given, spare = [largest] + [least] * (amount - 1), total - largest - least * (amount - 1)
    while spare > 0:
        candidates = [i for i in range(1, amount) if given[i] < largest] or [i for i in range(1, amount) if given[i] < reach]
        pool, left = sum([weights[i] for i in candidates]), spare
        for i in candidates:
            extra = min(reach - given[i], max(1, left * weights[i] // pool), spare)
            given[i] = given[i] + extra
            spare = spare - extra
    return np.array(given)


def gaussian(own_key, dims, deviation, bound, cuts=(), held_as=jnp.bfloat16):
    gain = steps_of(own_key, dims, cuts, -0.22, 0.18) if cuts else 1.0
    result = jax.random.normal(own_key, dims, jnp.float32) * deviation * gain
    return jnp.minimum(jnp.maximum(result, -bound), bound).astype(held_as)


def setup_inputs(seed: int = 0) -> dict:
    key_list = jax.random.split(jax.random.key(seed), 13)
    hidden_in = gaussian(key_list[0], (ROWS, D), 0.05, 0.29882812, ((0, 128),))
    queries = draw_queries(jax.random.fold_in(key_list[12], 71), 0)
    latent_cache = draw_latent_cache(jax.random.fold_in(key_list[12], 71), 0)
    cache_lengths = draw_cache_lengths(jax.random.fold_in(key_list[12], 71), 0)
    value_up = gaussian(key_list[4], (H, LAT, VH), LAT ** -0.5, 0.25, ((0, 128),))
    out_proj = gaussian(key_list[5], (H * VH, D), (H * VH) ** -0.5, 0.046875, ((0, 128),))
    norm_gain = jnp.clip(1.0 + 0.1 * jax.random.normal(key_list[6], (D,), jnp.float32), 0.5, 1.5)
    expert_ids_keys = jax.random.split(jax.random.fold_in(key_list[7], 1), ROWS // ROWS_DEV)
    expert_ids_turns = jax.random.permutation(jax.random.fold_in(key_list[7], 3), ROWS // ROWS_DEV)
    expert_ids = jax.vmap(lambda own, number: shared_out(jax.random.fold_in(key_list[7], 2), own, number, ROWS_DEV, EXPERTS, TOP, MOST, 2))(expert_ids_keys, expert_ids_turns).reshape((ROWS, TOP))
    route_weights = jnp.clip(0.1 + 0.4 * jax.random.uniform(key_list[8], (ROWS, TOP), jnp.float32) ** steps_of(key_list[8], (ROWS, TOP), ((0, 128),), -0.2, 0.2), 0.1, 0.5)
    w_gate = gaussian(key_list[9], (D, EXPERTS * FF), D ** -0.5, 0.0625, ((1, 128),))
    w_up = gaussian(key_list[10], (D, EXPERTS * FF), D ** -0.5, 0.0625, ((1, 128),))
    w_down = gaussian(key_list[11], (EXPERTS * FF, D), FF ** -0.5, 0.125, ((0, 128),))
    return dict(hidden_in=hidden_in, queries=queries, latent_cache=latent_cache, cache_lengths=cache_lengths, value_up=value_up, out_proj=out_proj, norm_gain=norm_gain, expert_ids=expert_ids, route_weights=route_weights, w_gate=w_gate, w_up=w_up, w_down=w_down)


score_scale = 0.07216878364870322

def attend_row(inputs):
    query, cache, length = inputs
    score = jnp.einsum('hc,lc->hl', query.astype(jnp.float32), cache.astype(jnp.float32)) * score_scale
    live = jnp.arange(LEN, dtype=jnp.int32) < length
    score = jnp.where(live[None, :], score, -1e+30)
    peak = lax.optimization_barrier(jnp.max(score, axis=-1))
    weight = jnp.where(live[None, :], jnp.exp(score - peak[:, None]), 0.0)
    total = lax.optimization_barrier(jnp.sum(weight, axis=-1))
    summed = jnp.dot(weight.astype(jnp.bfloat16), cache[:, :LAT], preferred_element_type=jnp.float32)
    return (summed / total[:, None]).astype(jnp.bfloat16)

def reference(hidden_in, queries, latent_cache, cache_lengths, value_up, out_proj, norm_gain, expert_ids, route_weights, w_gate, w_up, w_down):
    attended = lax.map(attend_row, (queries, latent_cache, cache_lengths))
    head_values = jnp.einsum('rhc,hcv->rhv', attended.astype(jnp.float32), value_up.astype(jnp.float32)).astype(jnp.bfloat16)
    attn_out = jnp.dot(head_values.reshape(ROWS, H * VH), out_proj, preferred_element_type=jnp.float32)
    resid = hidden_in.astype(jnp.float32) + attn_out
    mean_sq = lax.optimization_barrier(jnp.mean(resid * resid, axis=-1, keepdims=True))
    normed = (resid * lax.rsqrt(mean_sq + 1e-06) * norm_gain.astype(jnp.float32)).astype(jnp.bfloat16)
    named = expert_ids[:, :, None] == jnp.arange(EXPERTS, dtype=jnp.int32)[None, None, :]
    row_weight = lax.optimization_barrier(jnp.sum(jnp.where(named, route_weights[:, :, None], 0.0), axis=1))
    member = lax.optimization_barrier(jnp.sum(named.astype(jnp.int32), axis=1))
    pieces = N_SEC * N_DEV // EXPERTS
    piece_len = FF // pieces
    capacity = N_SEC * N_DEV * MOST

    def add_piece(index, total):
        expert = index // pieces
        start = (index * piece_len).astype(jnp.int32)
        gate_cols = lax.dynamic_slice_in_dim(w_gate, start, piece_len, 1)
        up_cols = lax.dynamic_slice_in_dim(w_up, start, piece_len, 1)
        down_rows = lax.dynamic_slice_in_dim(w_down, start, piece_len, 0)
        column = lax.dynamic_slice_in_dim(member, expert.astype(jnp.int32), 1, 1)[:, 0]
        order = jnp.argsort(1 - column, stable=True)[:capacity].astype(jnp.int32)
        chosen = normed[order]
        scales = lax.dynamic_slice_in_dim(row_weight, expert.astype(jnp.int32), 1, 1)[order]
        gate = jnp.dot(chosen, gate_cols, preferred_element_type=jnp.float32)
        upper = jnp.dot(chosen, up_cols, preferred_element_type=jnp.float32)
        part_hidden = (jax.nn.silu(gate) * upper).astype(jnp.bfloat16)
        part_out = jnp.dot(part_hidden, down_rows, preferred_element_type=jnp.float32).astype(jnp.bfloat16)
        return total.at[order].add(scales * part_out.astype(jnp.float32))
    expert_sum = lax.fori_loop(0, EXPERTS * pieces, add_piece, jnp.zeros((ROWS, D), jnp.float32))
    return (resid + expert_sum).astype(jnp.bfloat16)
```

```python
import jax
import jax.numpy as jnp
from jax import lax
from jax.experimental import pallas as pl
from jax.experimental.pallas import tpu as pltpu
from jax.sharding import PartitionSpec as P

EXPERTS = 16
ROWS_DEV = 2
MESH = pl.DeviceIdType.MESH
F32 = jnp.float32
BF16 = jnp.bfloat16
MIB = 2**20

score_scale = 0.07216878364870322

TILES = (19, 19, 18)
WIDE = 19 * 128
STARTS = (0, 2432, 4864)
WIDTHS = (2432, 2432, 2304)
SUB = 24


def dev_of(part, g, o):
    if part == 0:
        return g * 16 + o
    if part == 1:
        return (o // 4) * 16 + g * 4 + o % 4
    return o * 4 + g


def place_of(part, dev):
    if part == 0:
        return dev // 16, dev % 16
    if part == 1:
        return (dev // 4) % 4, (dev // 16) * 4 + dev % 4
    return dev % 4, dev // 4


def attend_kernel(lengths_ref, queries_ref, cache_ref, out_ref, score_ref, weight_ref, spread_ref):
    row = pl.program_id(0)
    length = lengths_ref[row]
    span = cache_ref.shape[1]
    block = 512
    query = queries_ref[0]
    peak = jnp.full((128, 1), -1e30, F32)
    for start in range(0, span, block):
        score = lax.dot_general(
            query,
            cache_ref[0, start : start + block, :],
            (((1,), (1,)), ((), ())),
            preferred_element_type=F32,
        )
        position = start + lax.broadcasted_iota(jnp.int32, (1, block), 1)
        score = jnp.where(position < length, score * score_scale, -1e30)
        score_ref[:, start : start + block] = score
        peak = jnp.maximum(peak, jnp.max(score, axis=1, keepdims=True))
    total = jnp.zeros((128, 1), F32)
    for start in range(0, span, block):
        weight = jnp.exp(score_ref[:, start : start + block] - peak)
        total = total + jnp.sum(weight, axis=1, keepdims=True)
        weight_ref[:, start : start + block] = weight.astype(BF16)
    summed = jnp.dot(weight_ref[...], cache_ref[0, :, 0:512], preferred_element_type=F32)
    attended = summed / total
    for half in range(2):
        for chunk in range(4):
            spread_ref[pl.ds(half * 4 + chunk, 64, stride=8), :] = attended[
                half * 64 : half * 64 + 64, chunk * 128 : chunk * 128 + 128
            ]
    out_ref[0] = spread_ref[...].astype(BF16)


def attend(queries, latent_cache, cache_lengths):
    rows, heads, depth = queries.shape
    span = latent_cache.shape[1]
    return pl.pallas_call(
        attend_kernel,
        grid=(rows,),
        out_shape=jax.ShapeDtypeStruct((rows, 512, 128), BF16),
        in_specs=[
            pl.BlockSpec(memory_space=pltpu.SMEM),
            pl.BlockSpec((1, heads, depth), lambda r: (r, 0, 0)),
            pl.BlockSpec((1, span, depth), lambda r: (r, 0, 0)),
        ],
        out_specs=pl.BlockSpec((1, 512, 128), lambda r: (r, 0, 0)),
        scratch_shapes=[
            pltpu.VMEM((128, span), F32),
            pltpu.VMEM((128, span), BF16),
            pltpu.VMEM((512, 128), F32),
        ],
        compiler_params=pltpu.CompilerParams(vmem_limit_bytes=40 * MIB),
        name="attend",
    )(cache_lengths, queries, latent_cache)


def key_of(part, q):
    dev = dev_of(part, q // 32, q % 16)
    return ((q // 16) % 2) * 64 + dev


def one_hot(rows_key, cols_key):
    return jnp.where(rows_key == cols_key, 1.0, 0.0).astype(BF16)


def iota(axis, shape=(128, 128)):
    return lax.broadcasted_iota(jnp.int32, shape, axis)


def layer_kernel(
    att_ref,
    hidden_ref,
    ids_ref,
    route_ref,
    gain_ref,
    value_up_ref,
    out_proj_ref,
    w_gate_ref,
    w_up_ref,
    w_down_ref,
    out_ref,
    vu_buf,
    op_buf,
    wg_buf,
    wu_buf,
    wd_buf,
    msg_buf,
    by_head,
    spread,
    heads_buf,
    sums_out,
    sums_in,
    lanes,
    plane_out,
    plane_in,
    resid_buf,
    hidden_buf,
    gain_buf,
    normed_buf,
    gather_in,
    gather_out,
    rows_in,
    rows_all,
    back_out,
    back_in,
    plane_out2,
    plane_in2,
    load_sem,
    swap_send,
    swap_recv,
    a2a_send,
    a2a_recv,
    axis_send,
    axis_recv,
    plane_send,
    plane_recv,
):
    sec = lax.axis_index("sec")
    me = lax.axis_index("dev")
    places = [place_of(part, me) for part in range(3)]

    barrier = pltpu.get_barrier_semaphore()

    def greet(step, carry):
        pl.semaphore_signal(
            barrier, inc=1, device_id=(sec, lax.rem(me + step, 64)), device_id_type=MESH
        )
        return carry

    lax.fori_loop(1, 64, greet, 0)
    pl.semaphore_signal(barrier, inc=1, device_id=(1 - sec, me), device_id_type=MESH)

    weights = (
        (value_up_ref, vu_buf),
        (out_proj_ref, op_buf),
        (w_gate_ref, wg_buf),
        (w_up_ref, wu_buf),
        (w_down_ref, wd_buf),
    )
    loads = [
        pltpu.make_async_copy(source, target.at[sec], load_sem.at[index])
        for index, (source, target) in enumerate(weights)
    ]
    swaps = [
        pltpu.make_async_remote_copy(
            source,
            target.at[sec],
            swap_send.at[index],
            swap_recv.at[index],
            device_id=(1 - sec, me),
            device_id_type=MESH,
        )
        for index, (source, target) in enumerate(weights)
    ]
    for load in loads:
        load.start()

    for index in range(64):
        msg_buf[index] = jnp.concatenate(
            [att_ref[row, index * 8 : index * 8 + 8, :].astype(F32) for row in range(ROWS_DEV)]
        ).astype(BF16)

    pl.semaphore_wait(barrier, 64)
    swaps[0].start()
    swaps[1].start()

    def send_attended(step, carry):
        peer = lax.rem(me + step, 64)
        pltpu.make_async_remote_copy(
            msg_buf.at[peer],
            by_head.at[me],
            a2a_send,
            a2a_recv,
            device_id=(sec, peer),
            device_id_type=MESH,
        ).start()
        return carry

    lax.fori_loop(1, 64, send_attended, 0)
    for swap in swaps[2:]:
        swap.start()
    by_head[me] = msg_buf[me]

    lanes[...] = jnp.zeros(lanes.shape, F32)
    hidden_buf[...] = jnp.zeros(hidden_buf.shape, F32)
    gain_buf[...] = jnp.zeros(gain_buf.shape, F32)
    hidden = hidden_ref[...].astype(F32)
    gains = gain_ref[...]
    for part in range(3):
        for tile in range(TILES[part]):
            column = STARTS[part] + tile * 128
            for row in range(ROWS_DEV):
                at = row * SUB + tile
                hidden_buf[part, at : at + 1, :] = hidden[row : row + 1, column : column + 128]
                gain_buf[part, at : at + 1, :] = gains[:, column : column + 128]

    a2a_all = pltpu.make_async_remote_copy(
        msg_buf.at[pl.ds(0, 63)],
        by_head.at[pl.ds(0, 63)],
        a2a_send,
        a2a_recv,
        device_id=(sec, lax.rem(me + 1, 64)),
        device_id_type=MESH,
    )
    loads[0].wait()
    loads[1].wait()
    swaps[0].wait_recv()
    swaps[1].wait_recv()
    a2a_all.wait_recv()

    spread[...] = by_head[...].reshape(1024, 128).astype(F32)
    for half in range(2):
        parts = []
        for row in range(ROWS_DEV):
            parts.append(
                jnp.concatenate(
                    [
                        spread[pl.ds(row * 8 + half * 4 + chunk, 64, stride=16), :].astype(BF16)
                        for chunk in range(4)
                    ],
                    axis=1,
                )
            )
        heads_buf[:, half * 128 : half * 128 + 128] = jnp.dot(
            jnp.concatenate(parts), vu_buf[half], preferred_element_type=F32
        ).astype(BF16)

    def start_axis(part, source, target, phase):
        g, o = places[part]
        for step in (1, 3, 2):
            to = lax.rem(g + step, 4)
            pltpu.make_async_remote_copy(
                source.at[part, to],
                target.at[part, g],
                axis_send.at[phase, part],
                axis_recv.at[phase, part],
                device_id=(sec, dev_of(part, to, o)),
                device_id_type=MESH,
            ).start()

    def axis_all(part, source, target, phase):
        g, o = places[part]
        return pltpu.make_async_remote_copy(
            source.at[part, pl.ds(0, 3)],
            target.at[part, pl.ds(0, 3)],
            axis_send.at[phase, part],
            axis_recv.at[phase, part],
            device_id=(sec, dev_of(part, lax.rem(g + 1, 4), o)),
            device_id_type=MESH,
        )

    def start_plane(part, source_of, target, phase):
        g, o = places[part]

        def send(step, carry):
            to = lax.rem(o + step, 16)
            pltpu.make_async_remote_copy(
                source_of(to),
                target.at[part, o],
                plane_send.at[phase, part],
                plane_recv.at[phase, part],
                device_id=(sec, dev_of(part, g, to)),
                device_id_type=MESH,
            ).start()
            return carry

        lax.fori_loop(1, 16, send, 0)

    def plane_all(part, target, phase):
        g, o = places[part]
        whole = target.at[part, pl.ds(0, 15)]
        return pltpu.make_async_remote_copy(
            whole,
            whole,
            plane_send.at[phase, part],
            plane_recv.at[phase, part],
            device_id=(sec, dev_of(part, g, lax.rem(o + 1, 16))),
            device_id_type=MESH,
        )

    def reduce_axis(part, incoming, outgoing, phase, plane_phase, target):
        g, o = places[part]
        axis_all(part, outgoing, incoming, phase).wait_recv()
        for tile in range(TILES[part]):
            columns = slice(tile * 128, tile * 128 + 128)
            total = incoming[part, 0, :, columns].astype(F32)
            for slot in range(1, 4):
                total = total + incoming[part, slot, :, columns].astype(F32)
            for row in range(ROWS_DEV):
                lanes[part, pl.ds(row * SUB + tile, 16, stride=2 * SUB), :] = total[
                    row * 16 : row * 16 + 16
                ]
        buf = plane_out if plane_phase == 0 else plane_out2
        buf[part] = lanes[part].reshape(16, 2 * SUB, 128).astype(BF16)
        target[part, o] = buf[part, o]
        start_plane(part, lambda to: buf.at[part, to], target, plane_phase)

    def reduce_plane(part, target, plane_phase):
        plane_all(part, target, plane_phase).wait_recv()
        return jnp.sum(target[part].astype(F32), axis=0)

    rows_i, cols_i = iota(0), iota(1)
    for part in range(3):
        g, o = places[part]
        ordered = jnp.dot(
            one_hot(key_of(part, rows_i), cols_i), heads_buf[...], preferred_element_type=F32
        ).astype(BF16)
        columns = slice(STARTS[part], STARTS[part] + WIDTHS[part])
        product = jnp.dot(
            ordered[:, 0:128], op_buf[0, :, columns], preferred_element_type=F32
        ) + jnp.dot(ordered[:, 128:256], op_buf[1, :, columns], preferred_element_type=F32)
        sums_out[part, :, :, 0 : WIDTHS[part]] = product.astype(BF16).reshape(4, 32, WIDTHS[part])
        if WIDTHS[part] < WIDE:
            sums_out[part, :, :, WIDTHS[part] :] = jnp.zeros((4, 32, WIDE - WIDTHS[part]), BF16)
        start_axis(part, sums_out, sums_in, 0)
        sums_in[part, g] = sums_out[part, g]
    for part in range(3):
        reduce_axis(part, sums_in, sums_out, 0, 0, plane_in)
    square = [jnp.zeros((1, 1), F32) for row in range(ROWS_DEV)]
    for part in range(3):
        resid = hidden_buf[part] + reduce_plane(part, plane_in, 0)
        resid_buf[part] = resid
        for row in range(ROWS_DEV):
            piece = resid[row * SUB : row * SUB + SUB]
            square[row] = square[row] + jnp.sum(piece * piece, keepdims=True)

    lane = iota(1, (1, 128))
    routes = []
    for row in range(ROWS_DEV):
        dense = jnp.zeros((1, 128), F32)
        for slot in range(8):
            dense = dense + jnp.where(
                lane % EXPERTS == ids_ref[row, slot], route_ref[row, slot], 0.0
            )
        high = dense.astype(BF16).astype(F32)
        middle = (dense - high).astype(BF16).astype(F32)
        low = dense - high - middle
        routes.append(
            jnp.where(
                lane < 16,
                high,
                jnp.where(lane < 32, middle, jnp.where(lane < 48, low, 0.0)),
            )
        )
    for part in range(3):
        g, o = places[part]
        for row in range(ROWS_DEV):
            block = slice(row * SUB, row * SUB + SUB)
            scale = lax.rsqrt(square[row] / 7168.0 + 1e-06)
            normed_buf[part, block, :] = resid_buf[part, block, :] * scale * gain_buf[part, block, :]
            if part == 2:
                at = row * SUB + 18
                normed_buf[part, at : at + 1, :] = routes[row]
        gather_out[part] = normed_buf[part].astype(BF16)
        gather_in[part, o] = gather_out[part]
        start_plane(part, lambda to: gather_out.at[part], gather_in, 1)
    for part in range(3):
        g, o = places[part]
        plane_all(part, gather_in, 1).wait_recv()
        lanes[part] = gather_in[part].reshape(16 * 2 * SUB, 128).astype(F32)
        for tile in range(19):
            for row in range(ROWS_DEV):
                rows_in[part, g, row * 16 : row * 16 + 16, tile * 128 : tile * 128 + 128] = lanes[
                    part, pl.ds(row * SUB + tile, 16, stride=2 * SUB), :
                ].astype(BF16)
        for step in (1, 3, 2):
            to = lax.rem(g + step, 4)
            pltpu.make_async_remote_copy(
                rows_in.at[part, g],
                rows_in.at[part, g],
                axis_send.at[1, part],
                axis_recv.at[1, part],
                device_id=(sec, dev_of(part, to, o)),
                device_id_type=MESH,
            ).start()

    for index in range(2, 5):
        loads[index].wait()
        swaps[index].wait_recv()
    gate = [jnp.zeros((128, 256), F32) for piece in range(2)]
    upper = [jnp.zeros((128, 256), F32) for piece in range(2)]
    for part in range(3):
        axis_all(part, rows_in, rows_in, 1).wait_recv()
        block = rows_in[part].reshape(128, WIDE)
        if part > 0:
            block = jnp.dot(
                one_hot(key_of(0, rows_i), key_of(part, cols_i)), block, preferred_element_type=F32
            ).astype(BF16)
        if part == 2:
            named = block[:, 2304:2432]
            block = block[:, 0:2304]
        depth = slice(STARTS[part], STARTS[part] + WIDTHS[part])
        for piece in range(2):
            gate[piece] = gate[piece] + jnp.dot(
                block, wg_buf[piece, depth, :], preferred_element_type=F32
            )
            upper[piece] = upper[piece] + jnp.dot(
                block, wu_buf[piece, depth, :], preferred_element_type=F32
            )
    rows_all[:, 512:640] = named
    for piece in range(2):
        value = gate[piece]
        rows_all[:, piece * 256 : piece * 256 + 256] = (
            value / (1.0 + jnp.exp(-value)) * upper[piece]
        ).astype(BF16)
    expert_lane = iota(1)
    for part in range(3):
        g, o = places[part]
        if part == 0:
            hidden_units = rows_all[...]
        else:
            hidden_units = jnp.dot(
                one_hot(key_of(part, rows_i), key_of(0, cols_i)),
                rows_all[...],
                preferred_element_type=F32,
            ).astype(BF16)
        columns = slice(STARTS[part], STARTS[part] + WIDTHS[part])
        product = jnp.zeros((128, WIDTHS[part]), F32)
        for piece in range(2):
            expert = piece * 8 + me // 8
            mine = (expert_lane < 48) & (expert_lane % EXPERTS == expert)
            weight = jnp.sum(
                jnp.where(mine, hidden_units[:, 512:640].astype(F32), 0.0), axis=1, keepdims=True
            )
            product = product + weight * jnp.dot(
                hidden_units[:, piece * 256 : piece * 256 + 256],
                wd_buf[piece, :, columns],
                preferred_element_type=F32,
            )
        back_out[part, :, :, 0 : WIDTHS[part]] = product.astype(BF16).reshape(4, 32, WIDTHS[part])
        if WIDTHS[part] < WIDE:
            back_out[part, :, :, WIDTHS[part] :] = jnp.zeros((4, 32, WIDE - WIDTHS[part]), BF16)
        start_axis(part, back_out, back_in, 2)
        back_in[part, g] = back_out[part, g]
    for part in range(3):
        if part == 2:
            lanes[2] = jnp.zeros(lanes.shape[1:], F32)
        reduce_axis(part, back_in, back_out, 2, 2, plane_in2)
    for part in range(3):
        resid_buf[part] = resid_buf[part] + reduce_plane(part, plane_in2, 2)
        for tile in range(TILES[part]):
            column = STARTS[part] + tile * 128
            for row in range(ROWS_DEV):
                at = row * SUB + tile
                out_ref[row : row + 1, column : column + 128] = resid_buf[part, at : at + 1, :].astype(
                    BF16
                )

    for swap in swaps:
        swap.wait_send()
    a2a_all.wait_send()
    for part in range(3):
        axis_all(part, sums_out, sums_in, 0).wait_send()
        axis_all(part, rows_in, rows_in, 1).wait_send()
        axis_all(part, back_out, back_in, 2).wait_send()
        for phase, target in enumerate((plane_in, gather_in, plane_in2)):
            plane_all(part, target, phase).wait_send()


def layer(att, hidden_in, expert_ids, route_weights, norm_gain, value_up, out_proj, w_gate, w_up, w_down):
    vmem = pl.BlockSpec(memory_space=pltpu.VMEM)
    smem = pl.BlockSpec(memory_space=pltpu.SMEM)
    hbm = pl.BlockSpec(memory_space=pl.ANY)
    dma = pltpu.SemaphoreType.DMA
    return pl.pallas_call(
        layer_kernel,
        out_shape=jax.ShapeDtypeStruct((2, 7168), BF16),
        in_specs=[vmem, vmem, smem, smem, vmem, hbm, hbm, hbm, hbm, hbm],
        out_specs=vmem,
        scratch_shapes=[
            pltpu.VMEM((2, 512, 128), BF16),
            pltpu.VMEM((2, 128, 7168), BF16),
            pltpu.VMEM((2, 7168, 256), BF16),
            pltpu.VMEM((2, 7168, 256), BF16),
            pltpu.VMEM((2, 256, 7168), BF16),
            pltpu.VMEM((64, 16, 128), BF16),
            pltpu.VMEM((64, 16, 128), BF16),
            pltpu.VMEM((1024, 128), F32),
            pltpu.VMEM((128, 256), BF16),
            pltpu.VMEM((3, 4, 32, WIDE), BF16),
            pltpu.VMEM((3, 4, 32, WIDE), BF16),
            pltpu.VMEM((3, 16 * 2 * SUB, 128), F32),
            pltpu.VMEM((3, 16, 2 * SUB, 128), BF16),
            pltpu.VMEM((3, 16, 2 * SUB, 128), BF16),
            pltpu.VMEM((3, 2 * SUB, 128), F32),
            pltpu.VMEM((3, 2 * SUB, 128), F32),
            pltpu.VMEM((3, 2 * SUB, 128), F32),
            pltpu.VMEM((3, 2 * SUB, 128), F32),
            pltpu.VMEM((3, 16, 2 * SUB, 128), BF16),
            pltpu.VMEM((3, 2 * SUB, 128), BF16),
            pltpu.VMEM((3, 4, 32, WIDE), BF16),
            pltpu.VMEM((128, 640), BF16),
            pltpu.VMEM((3, 4, 32, WIDE), BF16),
            pltpu.VMEM((3, 4, 32, WIDE), BF16),
            pltpu.VMEM((3, 16, 2 * SUB, 128), BF16),
            pltpu.VMEM((3, 16, 2 * SUB, 128), BF16),
            dma((5,)),
            dma((5,)),
            dma((5,)),
            dma,
            dma,
            dma((3, 3)),
            dma((3, 3)),
            dma((3, 3)),
            dma((3, 3)),
        ],
        compiler_params=pltpu.CompilerParams(
            collective_id=0, has_side_effects=True, vmem_limit_bytes=58 * MIB
        ),
        name="layer",
    )(
        att,
        hidden_in,
        expert_ids,
        route_weights,
        norm_gain.reshape(1, -1),
        value_up.reshape(512, 128),
        out_proj,
        w_gate,
        w_up,
        w_down,
    )


def per_device(
    hidden_in,
    queries,
    latent_cache,
    cache_lengths,
    value_up,
    out_proj,
    norm_gain,
    expert_ids,
    route_weights,
    w_gate,
    w_up,
    w_down,
):
    att = attend(queries, latent_cache, cache_lengths)
    return layer(
        att, hidden_in, expert_ids, route_weights, norm_gain, value_up, out_proj, w_gate, w_up, w_down
    )


def solution(mesh):
    rows = P(("sec", "dev"), None)
    rows3 = P(("sec", "dev"), None, None)
    placed = (
        rows,
        rows3,
        rows3,
        P(("sec", "dev")),
        rows3,
        rows,
        P(),
        rows,
        rows,
        P(None, ("sec", "dev")),
        P(None, ("sec", "dev")),
        rows,
    )
    return jax.shard_map(
        per_device, mesh=mesh, in_specs=placed, out_specs=rows, check_vma=False
    )
```

```python
import jax
import jax.numpy as jnp
from jax import lax
from jax.experimental import pallas as pl
from jax.experimental.pallas import tpu as pltpu
from jax.sharding import PartitionSpec as P

EXPERTS = 16
ROWS_DEV = 2
MESH = pl.DeviceIdType.MESH
F32 = jnp.float32
BF16 = jnp.bfloat16
MIB = 2**20

score_scale = 0.07216878364870322

TILES = (19, 19, 18)
WIDE = 19 * 128
STARTS = (0, 2432, 4864)
WIDTHS = (2432, 2432, 2304)
SUB = 24


def dev_of(part, g, o):
    if part == 0:
        return g * 16 + o
    if part == 1:
        return (o // 4) * 16 + g * 4 + o % 4
    return o * 4 + g


def place_of(part, dev):
    if part == 0:
        return dev // 16, dev % 16
    if part == 1:
        return (dev // 4) % 4, (dev // 16) * 4 + dev % 4
    return dev % 4, dev // 4


def key_of(part, q):
    dev = dev_of(part, q // 32, q % 16)
    return ((q // 16) % 2) * 64 + dev


def one_hot(rows_key, cols_key):
    return jnp.where(rows_key == cols_key, 1.0, 0.0).astype(BF16)


def iota(axis, shape=(128, 128)):
    return lax.broadcasted_iota(jnp.int32, shape, axis)


def layer_kernel(
    lengths_ref,
    queries_ref,
    cache_ref,
    hidden_ref,
    ids_ref,
    route_ref,
    gain_ref,
    value_up_ref,
    out_proj_ref,
    w_gate_ref,
    w_up_ref,
    w_down_ref,
    out_ref,
    cache_buf,
    score_buf,
    weight_buf,
    vu_buf,
    op_buf,
    wg_buf,
    wu_buf,
    wd_buf,
    msg_buf,
    by_head,
    spread,
    heads_buf,
    sums_out,
    sums_in,
    lanes,
    plane_out,
    plane_in,
    resid_buf,
    hidden_buf,
    gain_buf,
    normed_buf,
    gather_in,
    gather_out,
    rows_in,
    rows_all,
    back_out,
    back_in,
    plane_out2,
    plane_in2,
    cache_sem,
    load_sem,
    swap_send,
    swap_recv,
    a2a_send,
    a2a_recv,
    axis_send,
    axis_recv,
    plane_send,
    plane_recv,
):
    sec = lax.axis_index("sec")
    me = lax.axis_index("dev")
    places = [place_of(part, me) for part in range(3)]

    barrier = pltpu.get_barrier_semaphore()

    def greet(step, carry):
        pl.semaphore_signal(
            barrier, inc=1, device_id=(sec, lax.rem(me + step, 64)), device_id_type=MESH
        )
        return carry

    def greet_all():
        lax.fori_loop(1, 64, greet, 0)
        pl.semaphore_signal(barrier, inc=1, device_id=(1 - sec, me), device_id_type=MESH)

    weights = (
        (value_up_ref, vu_buf),
        (out_proj_ref, op_buf),
        (w_gate_ref, wg_buf),
        (w_up_ref, wu_buf),
        (w_down_ref, wd_buf),
    )
    loads = [
        pltpu.make_async_copy(source, target.at[sec], load_sem.at[index])
        for index, (source, target) in enumerate(weights)
    ]
    swaps = [
        pltpu.make_async_remote_copy(
            source,
            target.at[sec],
            swap_send.at[index],
            swap_recv.at[index],
            device_id=(1 - sec, me),
            device_id_type=MESH,
        )
        for index, (source, target) in enumerate(weights)
    ]
    span, step_len = cache_ref.shape[2], 512
    cache_loads = [
        [
            pltpu.make_async_copy(
                cache_ref.at[row, :, pl.ds(start, step_len)],
                cache_buf.at[row, :, pl.ds(start, step_len)],
                cache_sem.at[row, start // step_len],
            )
            for start in range(0, span, step_len)
        ]
        for row in range(ROWS_DEV)
    ]
    for copy in cache_loads[0] + cache_loads[1]:
        copy.start()
    greet_all()

    for row in range(ROWS_DEV):
        length = lengths_ref[row]
        query = queries_ref[row].T
        peak = jnp.full((128, 1), -1e30, F32)
        for start in range(0, span, step_len):
            cache_loads[row][start // step_len].wait()
            score = jnp.dot(
                query, cache_buf[row, :, start : start + step_len], preferred_element_type=F32
            )
            position = start + iota(1, (1, step_len))
            score = jnp.where(position < length, score * score_scale, -1e30)
            score_buf[:, start : start + step_len] = score
            peak = jnp.maximum(peak, jnp.max(score, axis=1, keepdims=True))
        total = jnp.zeros((128, 1), F32)
        for start in range(0, span, step_len):
            weight = jnp.exp(score_buf[:, start : start + step_len] - peak)
            total = total + jnp.sum(weight, axis=1, keepdims=True)
            weight_buf[:, start : start + step_len] = weight.astype(BF16)
        if row == 0:
            for load in loads:
                load.start()
            pl.semaphore_wait(barrier, 64)
            swaps[0].start()
            swaps[1].start()
        summed = lax.dot_general(
            weight_buf[...],
            cache_buf[row, 0:512, :],
            (((1,), (1,)), ((), ())),
            preferred_element_type=F32,
        )
        attended = summed / total
        for half in range(2):
            for chunk in range(4):
                spread[pl.ds(row * 8 + half * 4 + chunk, 64, stride=16), :] = attended[
                    half * 64 : half * 64 + 64, chunk * 128 : chunk * 128 + 128
                ]
    msg_buf[...] = spread[...].astype(BF16).reshape(64, 16, 128)

    def send_attended(step, carry):
        peer = lax.rem(me + step, 64)
        pltpu.make_async_remote_copy(
            msg_buf.at[peer],
            by_head.at[me],
            a2a_send,
            a2a_recv,
            device_id=(sec, peer),
            device_id_type=MESH,
        ).start()
        return carry

    lax.fori_loop(1, 64, send_attended, 0)
    for swap in swaps[2:]:
        swap.start()
    by_head[me] = msg_buf[me]

    lanes[...] = jnp.zeros(lanes.shape, F32)
    hidden_buf[...] = jnp.zeros(hidden_buf.shape, F32)
    gain_buf[...] = jnp.zeros(gain_buf.shape, F32)
    hidden = hidden_ref[...].astype(F32)
    gains = gain_ref[...]
    for part in range(3):
        for tile in range(TILES[part]):
            column = STARTS[part] + tile * 128
            for row in range(ROWS_DEV):
                at = row * SUB + tile
                hidden_buf[part, at : at + 1, :] = hidden[row : row + 1, column : column + 128]
                gain_buf[part, at : at + 1, :] = gains[:, column : column + 128]

    a2a_all = pltpu.make_async_remote_copy(
        msg_buf.at[pl.ds(0, 63)],
        by_head.at[pl.ds(0, 63)],
        a2a_send,
        a2a_recv,
        device_id=(sec, lax.rem(me + 1, 64)),
        device_id_type=MESH,
    )
    loads[0].wait()
    loads[1].wait()
    swaps[0].wait_recv()
    swaps[1].wait_recv()
    a2a_all.wait_recv()

    spread[...] = by_head[...].reshape(1024, 128).astype(F32)
    for half in range(2):
        parts = []
        for row in range(ROWS_DEV):
            parts.append(
                jnp.concatenate(
                    [
                        spread[pl.ds(row * 8 + half * 4 + chunk, 64, stride=16), :].astype(BF16)
                        for chunk in range(4)
                    ],
                    axis=1,
                )
            )
        heads_buf[:, half * 128 : half * 128 + 128] = jnp.dot(
            jnp.concatenate(parts), vu_buf[half], preferred_element_type=F32
        ).astype(BF16)

    def start_axis(part, source, target, phase):
        g, o = places[part]
        for step in (1, 3, 2):
            to = lax.rem(g + step, 4)
            pltpu.make_async_remote_copy(
                source.at[part, to],
                target.at[part, g],
                axis_send.at[phase, part],
                axis_recv.at[phase, part],
                device_id=(sec, dev_of(part, to, o)),
                device_id_type=MESH,
            ).start()

    def axis_all(part, source, target, phase):
        g, o = places[part]
        return pltpu.make_async_remote_copy(
            source.at[part, pl.ds(0, 3)],
            target.at[part, pl.ds(0, 3)],
            axis_send.at[phase, part],
            axis_recv.at[phase, part],
            device_id=(sec, dev_of(part, lax.rem(g + 1, 4), o)),
            device_id_type=MESH,
        )

    def start_plane(part, source_of, target, phase):
        g, o = places[part]

        def send(step, carry):
            to = lax.rem(o + step, 16)
            pltpu.make_async_remote_copy(
                source_of(to),
                target.at[part, o],
                plane_send.at[phase, part],
                plane_recv.at[phase, part],
                device_id=(sec, dev_of(part, g, to)),
                device_id_type=MESH,
            ).start()
            return carry

        lax.fori_loop(1, 16, send, 0)

    def plane_all(part, target, phase):
        g, o = places[part]
        whole = target.at[part, pl.ds(0, 15)]
        return pltpu.make_async_remote_copy(
            whole,
            whole,
            plane_send.at[phase, part],
            plane_recv.at[phase, part],
            device_id=(sec, dev_of(part, g, lax.rem(o + 1, 16))),
            device_id_type=MESH,
        )

    def reduce_axis(part, incoming, outgoing, phase, plane_phase, target):
        g, o = places[part]
        axis_all(part, outgoing, incoming, phase).wait_recv()
        for tile in range(TILES[part]):
            columns = slice(tile * 128, tile * 128 + 128)
            total = incoming[part, 0, :, columns].astype(F32)
            for slot in range(1, 4):
                total = total + incoming[part, slot, :, columns].astype(F32)
            for row in range(ROWS_DEV):
                lanes[part, pl.ds(row * SUB + tile, 16, stride=2 * SUB), :] = total[
                    row * 16 : row * 16 + 16
                ]
        buf = plane_out if plane_phase == 0 else plane_out2
        buf[part] = lanes[part].reshape(16, 2 * SUB, 128).astype(BF16)
        target[part, o] = buf[part, o]
        start_plane(part, lambda to: buf.at[part, to], target, plane_phase)

    def reduce_plane(part, target, plane_phase):
        plane_all(part, target, plane_phase).wait_recv()
        return jnp.sum(target[part].astype(F32), axis=0)

    rows_i, cols_i = iota(0), iota(1)
    for part in range(3):
        g, o = places[part]
        ordered = jnp.dot(
            one_hot(key_of(part, rows_i), cols_i), heads_buf[...], preferred_element_type=F32
        ).astype(BF16)
        columns = slice(STARTS[part], STARTS[part] + WIDTHS[part])
        product = jnp.dot(
            ordered[:, 0:128], op_buf[0, :, columns], preferred_element_type=F32
        ) + jnp.dot(ordered[:, 128:256], op_buf[1, :, columns], preferred_element_type=F32)
        sums_out[part, :, :, 0 : WIDTHS[part]] = product.astype(BF16).reshape(4, 32, WIDTHS[part])
        if WIDTHS[part] < WIDE:
            sums_out[part, :, :, WIDTHS[part] :] = jnp.zeros((4, 32, WIDE - WIDTHS[part]), BF16)
        start_axis(part, sums_out, sums_in, 0)
        sums_in[part, g] = sums_out[part, g]
    for part in range(3):
        reduce_axis(part, sums_in, sums_out, 0, 0, plane_in)
    square = [jnp.zeros((1, 1), F32) for row in range(ROWS_DEV)]
    for part in range(3):
        resid = hidden_buf[part] + reduce_plane(part, plane_in, 0)
        resid_buf[part] = resid
        for row in range(ROWS_DEV):
            piece = resid[row * SUB : row * SUB + SUB]
            square[row] = square[row] + jnp.sum(piece * piece, keepdims=True)

    lane = iota(1, (1, 128))
    routes = []
    for row in range(ROWS_DEV):
        dense = jnp.zeros((1, 128), F32)
        for slot in range(8):
            dense = dense + jnp.where(
                lane % EXPERTS == ids_ref[row, slot], route_ref[row, slot], 0.0
            )
        high = dense.astype(BF16).astype(F32)
        middle = (dense - high).astype(BF16).astype(F32)
        low = dense - high - middle
        routes.append(
            jnp.where(
                lane < 16,
                high,
                jnp.where(lane < 32, middle, jnp.where(lane < 48, low, 0.0)),
            )
        )
    for part in range(3):
        g, o = places[part]
        for row in range(ROWS_DEV):
            block = slice(row * SUB, row * SUB + SUB)
            scale = lax.rsqrt(square[row] / 7168.0 + 1e-06)
            normed_buf[part, block, :] = resid_buf[part, block, :] * scale * gain_buf[part, block, :]
            if part == 2:
                at = row * SUB + 18
                normed_buf[part, at : at + 1, :] = routes[row]
        gather_out[part] = normed_buf[part].astype(BF16)
        gather_in[part, o] = gather_out[part]
        start_plane(part, lambda to: gather_out.at[part], gather_in, 1)
    for part in range(3):
        g, o = places[part]
        plane_all(part, gather_in, 1).wait_recv()
        lanes[part] = gather_in[part].reshape(16 * 2 * SUB, 128).astype(F32)
        for tile in range(19):
            for row in range(ROWS_DEV):
                rows_in[part, g, row * 16 : row * 16 + 16, tile * 128 : tile * 128 + 128] = lanes[
                    part, pl.ds(row * SUB + tile, 16, stride=2 * SUB), :
                ].astype(BF16)
        for step in (1, 3, 2):
            to = lax.rem(g + step, 4)
            pltpu.make_async_remote_copy(
                rows_in.at[part, g],
                rows_in.at[part, g],
                axis_send.at[1, part],
                axis_recv.at[1, part],
                device_id=(sec, dev_of(part, to, o)),
                device_id_type=MESH,
            ).start()

    for index in range(2, 5):
        loads[index].wait()
        swaps[index].wait_recv()
    gate = [jnp.zeros((128, 256), F32) for piece in range(2)]
    upper = [jnp.zeros((128, 256), F32) for piece in range(2)]
    for part in range(3):
        axis_all(part, rows_in, rows_in, 1).wait_recv()
        block = rows_in[part].reshape(128, WIDE)
        if part > 0:
            block = jnp.dot(
                one_hot(key_of(0, rows_i), key_of(part, cols_i)), block, preferred_element_type=F32
            ).astype(BF16)
        if part == 2:
            named = block[:, 2304:2432]
            block = block[:, 0:2304]
        depth = slice(STARTS[part], STARTS[part] + WIDTHS[part])
        for piece in range(2):
            gate[piece] = gate[piece] + jnp.dot(
                block, wg_buf[piece, depth, :], preferred_element_type=F32
            )
            upper[piece] = upper[piece] + jnp.dot(
                block, wu_buf[piece, depth, :], preferred_element_type=F32
            )
    rows_all[:, 512:640] = named
    for piece in range(2):
        value = gate[piece]
        rows_all[:, piece * 256 : piece * 256 + 256] = (
            value / (1.0 + jnp.exp(-value)) * upper[piece]
        ).astype(BF16)
    expert_lane = iota(1)
    for part in range(3):
        g, o = places[part]
        if part == 0:
            hidden_units = rows_all[...]
        else:
            hidden_units = jnp.dot(
                one_hot(key_of(part, rows_i), key_of(0, cols_i)),
                rows_all[...],
                preferred_element_type=F32,
            ).astype(BF16)
        columns = slice(STARTS[part], STARTS[part] + WIDTHS[part])
        product = jnp.zeros((128, WIDTHS[part]), F32)
        for piece in range(2):
            expert = piece * 8 + me // 8
            mine = (expert_lane < 48) & (expert_lane % EXPERTS == expert)
            weight = jnp.sum(
                jnp.where(mine, hidden_units[:, 512:640].astype(F32), 0.0), axis=1, keepdims=True
            )
            product = product + weight * jnp.dot(
                hidden_units[:, piece * 256 : piece * 256 + 256],
                wd_buf[piece, :, columns],
                preferred_element_type=F32,
            )
        back_out[part, :, :, 0 : WIDTHS[part]] = product.astype(BF16).reshape(4, 32, WIDTHS[part])
        if WIDTHS[part] < WIDE:
            back_out[part, :, :, WIDTHS[part] :] = jnp.zeros((4, 32, WIDE - WIDTHS[part]), BF16)
        start_axis(part, back_out, back_in, 2)
        back_in[part, g] = back_out[part, g]
    for part in range(3):
        if part == 2:
            lanes[2] = jnp.zeros(lanes.shape[1:], F32)
        reduce_axis(part, back_in, back_out, 2, 2, plane_in2)
    for part in range(3):
        resid_buf[part] = resid_buf[part] + reduce_plane(part, plane_in2, 2)
        for tile in range(TILES[part]):
            column = STARTS[part] + tile * 128
            for row in range(ROWS_DEV):
                at = row * SUB + tile
                out_ref[row : row + 1, column : column + 128] = resid_buf[part, at : at + 1, :]

    for swap in swaps:
        swap.wait_send()
    a2a_all.wait_send()
    for part in range(3):
        axis_all(part, sums_out, sums_in, 0).wait_send()
        axis_all(part, rows_in, rows_in, 1).wait_send()
        axis_all(part, back_out, back_in, 2).wait_send()
        for phase, target in enumerate((plane_in, gather_in, plane_in2)):
            plane_all(part, target, phase).wait_send()


def layer(lengths, queries, cache, hidden_in, expert_ids, route_weights, norm_gain, value_up, out_proj, w_gate, w_up, w_down):
    vmem = pl.BlockSpec(memory_space=pltpu.VMEM)
    smem = pl.BlockSpec(memory_space=pltpu.SMEM)
    hbm = pl.BlockSpec(memory_space=pl.ANY)
    dma = pltpu.SemaphoreType.DMA
    return pl.pallas_call(
        layer_kernel,
        out_shape=jax.ShapeDtypeStruct((2, 7168), F32),
        in_specs=[smem, vmem, hbm, vmem, smem, smem, vmem, hbm, hbm, hbm, hbm, hbm],
        out_specs=vmem,
        scratch_shapes=[
            pltpu.VMEM((2, 576, 2048), BF16),
            pltpu.VMEM((128, 2048), F32),
            pltpu.VMEM((128, 2048), BF16),
            pltpu.VMEM((2, 512, 128), BF16),
            pltpu.VMEM((2, 128, 7168), BF16),
            pltpu.VMEM((2, 7168, 256), BF16),
            pltpu.VMEM((2, 7168, 256), BF16),
            pltpu.VMEM((2, 256, 7168), BF16),
            pltpu.VMEM((64, 16, 128), BF16),
            pltpu.VMEM((64, 16, 128), BF16),
            pltpu.VMEM((1024, 128), F32),
            pltpu.VMEM((128, 256), BF16),
            pltpu.VMEM((3, 4, 32, WIDE), BF16),
            pltpu.VMEM((3, 4, 32, WIDE), BF16),
            pltpu.VMEM((3, 16 * 2 * SUB, 128), F32),
            pltpu.VMEM((3, 16, 2 * SUB, 128), BF16),
            pltpu.VMEM((3, 16, 2 * SUB, 128), BF16),
            pltpu.VMEM((3, 2 * SUB, 128), F32),
            pltpu.VMEM((3, 2 * SUB, 128), F32),
            pltpu.VMEM((3, 2 * SUB, 128), F32),
            pltpu.VMEM((3, 2 * SUB, 128), F32),
            pltpu.VMEM((3, 16, 2 * SUB, 128), BF16),
            pltpu.VMEM((3, 2 * SUB, 128), BF16),
            pltpu.VMEM((3, 4, 32, WIDE), BF16),
            pltpu.VMEM((128, 640), BF16),
            pltpu.VMEM((3, 4, 32, WIDE), BF16),
            pltpu.VMEM((3, 4, 32, WIDE), BF16),
            pltpu.VMEM((3, 16, 2 * SUB, 128), BF16),
            pltpu.VMEM((3, 16, 2 * SUB, 128), BF16),
            dma((2, 4)),
            dma((5,)),
            dma((5,)),
            dma((5,)),
            dma,
            dma,
            dma((3, 3)),
            dma((3, 3)),
            dma((3, 3)),
            dma((3, 3)),
        ],
        compiler_params=pltpu.CompilerParams(
            collective_id=0, has_side_effects=True, vmem_limit_bytes=58 * MIB
        ),
        name="layer",
    )(
        lengths,
        queries,
        cache,
        hidden_in,
        expert_ids,
        route_weights,
        norm_gain.reshape(1, -1),
        value_up.reshape(512, 128),
        out_proj,
        w_gate,
        w_up,
        w_down,
    )


def per_device(
    hidden_in,
    queries,
    latent_cache,
    cache_lengths,
    value_up,
    out_proj,
    norm_gain,
    expert_ids,
    route_weights,
    w_gate,
    w_up,
    w_down,
):
    out = layer(
        cache_lengths,
        queries.transpose(0, 2, 1),
        latent_cache.transpose(0, 2, 1),
        hidden_in,
        expert_ids,
        route_weights,
        norm_gain,
        value_up,
        out_proj,
        w_gate,
        w_up,
        w_down,
    )
    return out.astype(BF16)


def solution(mesh):
    rows = P(("sec", "dev"), None)
    rows3 = P(("sec", "dev"), None, None)
    placed = (
        rows,
        rows3,
        rows3,
        P(("sec", "dev")),
        rows3,
        rows,
        P(),
        rows,
        rows,
        P(None, ("sec", "dev")),
        P(None, ("sec", "dev")),
        rows,
    )
    return jax.shard_map(
        per_device, mesh=mesh, in_specs=placed, out_specs=rows, check_vma=False
    )
```

```python
import jax
import jax.numpy as jnp
from jax import lax
from jax.experimental import pallas as pl
from jax.experimental.pallas import tpu as pltpu
from jax.sharding import PartitionSpec as P

EXPERTS = 16
ROWS_DEV = 2
MESH = pl.DeviceIdType.MESH
F32 = jnp.float32
BF16 = jnp.bfloat16
MIB = 2**20

score_scale = 0.07216878364870322

TILES = (11, 11, 10, 8, 8, 8, 1)
SUBS = (16, 16, 16, 8, 8, 8, 8)
FIRST = (0, 11, 22, 32, 40, 48)
CHUNKS = 6
WAVES = ((0, 1, 2), (3, 4, 5))
RING = (0, 1, 2, 1)
FAR_FIRST = sorted(
    [(x, z, y) for x in range(4) for z in range(4) for y in range(4)][1:],
    key=lambda at: -RING[at[0]] - RING[at[1]] - RING[at[2]],
)


def columns_of(chunk):
    return slice(FIRST[chunk] * 128, (FIRST[chunk] + TILES[chunk]) * 128)


class Axis:
    def __init__(self, kind):
        self.kind = kind
        self.first = (16, 4, 1)[kind]
        self.high = (4, 16, 16)[kind]
        self.low = (1, 1, 4)[kind]

    def dev(self, g, o):
        return g * self.first + (o // 4) * self.high + (o % 4) * self.low

    def place(self, dev):
        return (dev // self.first) % 4, (dev // self.high) % 4 * 4 + (dev // self.low) % 4

    def key(self, q):
        return ((q // 16) % 2) * 64 + self.dev(q // 32, q % 16)


def one_hot(rows_key, cols_key):
    return jnp.where(rows_key == cols_key, 1.0, 0.0).astype(BF16)


def iota(axis, shape=(128, 128)):
    return lax.broadcasted_iota(jnp.int32, shape, axis)


def three_terms(value):
    high = value.astype(BF16).astype(F32)
    middle = (value - high).astype(BF16).astype(F32)
    return high, middle, value - high - middle


def layer_kernel(
    lengths_ref,
    queries_ref,
    cache_ref,
    hidden_ref,
    ids_ref,
    route_ref,
    gain_ref,
    value_up_ref,
    out_proj_ref,
    w_gate_ref,
    w_up_ref,
    w_down_ref,
    out_ref,
    query_buf,
    hidden_rows,
    gain_row,
    cache_buf,
    score_buf,
    weight_buf,
    vu_buf,
    op_buf,
    wg_buf,
    wu_buf,
    wd_buf,
    msg_buf,
    by_head,
    spread,
    heads_buf,
    sums_out,
    sums_in,
    lanes,
    plane_out,
    plane_in,
    resid_buf,
    hidden_buf,
    gain_buf,
    gather_in,
    gather_out,
    rows_in,
    rows_all,
    heads_by_axis,
    units_by_axis,
    weight_by_axis,
    back_out,
    back_in,
    plane_out2,
    plane_in2,
    small_sem,
    cache_sem,
    load_sem,
    swap_send,
    swap_recv,
    a2a_send,
    a2a_recv,
    axis_send,
    axis_recv,
    plane_send,
    plane_recv,
):
    sec = lax.axis_index("sec")
    me = lax.axis_index("dev")
    axes = [Axis(kind) for kind in (0, 1, 2, 0, 1, 2, 2)]
    places = [axis.place(me) for axis in axes]

    barrier = pltpu.get_barrier_semaphore()

    def greet(step, carry):
        pl.semaphore_signal(
            barrier, inc=1, device_id=(sec, lax.rem(me + step, 64)), device_id_type=MESH
        )
        return carry

    def greet_all():
        lax.fori_loop(1, 64, greet, 0)
        pl.semaphore_signal(barrier, inc=1, device_id=(1 - sec, me), device_id_type=MESH)

    weights = (
        (value_up_ref, vu_buf),
        (out_proj_ref, op_buf),
        (w_gate_ref, wg_buf),
        (w_up_ref, wu_buf),
        (w_down_ref, wd_buf),
    )
    loads = [
        pltpu.make_async_copy(source, target.at[sec], load_sem.at[index])
        for index, (source, target) in enumerate(weights)
    ]
    swaps = [
        pltpu.make_async_remote_copy(
            source,
            target.at[sec],
            swap_send.at[index],
            swap_recv.at[index],
            device_id=(1 - sec, me),
            device_id_type=MESH,
        )
        for index, (source, target) in enumerate(weights)
    ]
    span, step_len = cache_ref.shape[2], 512
    cache_loads = [
        [
            pltpu.make_async_copy(
                cache_ref.at[row, :, pl.ds(start, step_len)],
                cache_buf.at[row, :, pl.ds(start, step_len)],
                cache_sem.at[row, start // step_len],
            )
            for start in range(0, span, step_len)
        ]
        for row in range(ROWS_DEV)
    ]
    small_loads = [
        pltpu.make_async_copy(source, target, small_sem.at[index])
        for index, (source, target) in enumerate(
            ((queries_ref, query_buf), (hidden_ref, hidden_rows), (gain_ref, gain_row))
        )
    ]
    small_loads[0].start()
    for copy in cache_loads[0] + cache_loads[1] + small_loads[1:]:
        copy.start()
    greet_all()
    small_loads[0].wait()

    for row in range(ROWS_DEV):
        length = lengths_ref[row]
        query = query_buf[row].T
        peak = jnp.full((128, 1), -1e30, F32)
        for start in range(0, span, step_len):
            cache_loads[row][start // step_len].wait()
            score = jnp.dot(
                query, cache_buf[row, :, start : start + step_len], preferred_element_type=F32
            )
            position = start + iota(1, (1, step_len))
            score = jnp.where(position < length, score * score_scale, -1e30)
            score_buf[:, start : start + step_len] = score
            peak = jnp.maximum(peak, jnp.max(score, axis=1, keepdims=True))
        total = jnp.zeros((128, 1), F32)
        for start in range(0, span, step_len):
            weight = jnp.exp(score_buf[:, start : start + step_len] - peak)
            total = total + jnp.sum(weight, axis=1, keepdims=True)
            weight_buf[:, start : start + step_len] = weight.astype(BF16)
        if row == 0:
            for load in loads:
                load.start()
            pl.semaphore_wait(barrier, 64)
            swaps[0].start()
            swaps[1].start()
        summed = lax.dot_general(
            weight_buf[...],
            cache_buf[row, 0:512, :],
            (((1,), (1,)), ((), ())),
            preferred_element_type=F32,
        )
        attended = summed / total
        for half in range(2):
            for chunk in range(4):
                spread[pl.ds(row * 8 + half * 4 + chunk, 64, stride=16), :] = attended[
                    half * 64 : half * 64 + 64, chunk * 128 : chunk * 128 + 128
                ]
    msg_buf[...] = spread[...].astype(BF16).reshape(64, 16, 128)

    for x, z, y in FAR_FIRST:
        peer = (me // 16 + x) % 4 * 16 + (me // 4 % 4 + z) % 4 * 4 + (me + y) % 4
        pltpu.make_async_remote_copy(
            msg_buf.at[peer],
            by_head.at[me],
            a2a_send,
            a2a_recv,
            device_id=(sec, peer),
            device_id_type=MESH,
        ).start()
    for swap in swaps[2:]:
        swap.start()
    by_head[me] = msg_buf[me]

    small_loads[1].wait()
    small_loads[2].wait()
    hidden = hidden_rows[...].astype(F32)
    gains = gain_row[...]
    for chunk in range(CHUNKS):
        hidden_buf[chunk][...] = jnp.zeros(hidden_buf[chunk].shape, F32)
        gain_buf[chunk][...] = jnp.zeros(gain_buf[chunk].shape, F32)
        lanes[chunk][...] = jnp.zeros(lanes[chunk].shape, F32)
        for tile in range(TILES[chunk]):
            column = (FIRST[chunk] + tile) * 128
            for row in range(ROWS_DEV):
                at = row * SUBS[chunk] + tile
                hidden_buf[chunk][at : at + 1, :] = hidden[row : row + 1, column : column + 128]
                gain_buf[chunk][at : at + 1, :] = gains[:, column : column + 128]

    a2a_all = pltpu.make_async_remote_copy(
        msg_buf.at[pl.ds(0, 63)],
        by_head.at[pl.ds(0, 63)],
        a2a_send,
        a2a_recv,
        device_id=(sec, lax.rem(me + 1, 64)),
        device_id_type=MESH,
    )
    loads[0].wait()
    loads[1].wait()
    swaps[0].wait_recv()
    swaps[1].wait_recv()
    a2a_all.wait_recv()

    spread[...] = by_head[...].reshape(1024, 128).astype(F32)
    for half in range(2):
        parts = []
        for row in range(ROWS_DEV):
            parts.append(
                jnp.concatenate(
                    [
                        spread[pl.ds(row * 8 + half * 4 + chunk, 64, stride=16), :].astype(BF16)
                        for chunk in range(4)
                    ],
                    axis=1,
                )
            )
        heads_buf[:, half * 128 : half * 128 + 128] = jnp.dot(
            jnp.concatenate(parts), vu_buf[half], preferred_element_type=F32
        ).astype(BF16)

    rows_i, cols_i = iota(0), iota(1)
    for kind in range(3):
        heads_by_axis[kind] = jnp.dot(
            one_hot(Axis(kind).key(rows_i), cols_i), heads_buf[...], preferred_element_type=F32
        ).astype(BF16)

    def axis_copy(chunk, source, target, phase, to):
        axis = axes[chunk]
        return pltpu.make_async_remote_copy(
            source,
            target,
            axis_send.at[phase, chunk],
            axis_recv.at[phase, chunk],
            device_id=(sec, axis.dev(to, places[chunk][1])),
            device_id_type=MESH,
        )

    def axis_all(chunk, target, phase):
        whole = target[chunk].at[pl.ds(0, 3)]
        return axis_copy(chunk, whole, whole, phase, lax.rem(places[chunk][0] + 1, 4))

    def start_reduce(chunk, outgoing, incoming, phase):
        g, o = places[chunk]
        for step in (2, 1, 3):
            to = lax.rem(g + step, 4)
            axis_copy(
                chunk, outgoing[chunk].at[to], incoming[chunk].at[g], phase, to
            ).start()
        incoming[chunk][g] = outgoing[chunk][g]

    def plane_copy(chunk, source, target, phase, to):
        return pltpu.make_async_remote_copy(
            source,
            target,
            plane_send.at[phase, chunk],
            plane_recv.at[phase, chunk],
            device_id=(sec, axes[chunk].dev(places[chunk][0], to)),
            device_id_type=MESH,
        )

    def plane_all(chunk, target, phase):
        whole = target[chunk].at[pl.ds(0, 15)]
        return plane_copy(chunk, whole, whole, phase, lax.rem(places[chunk][1] + 1, 16))

    def start_plane(chunk, source_of, target, phase):
        g, o = places[chunk]

        for x, high, low in FAR_FIRST:
            if x == 0:
                to = (o // 4 + high) % 4 * 4 + (o + low) % 4
                plane_copy(chunk, source_of(to), target[chunk].at[o], phase, to).start()

    def reduce_axis(chunk, incoming, outgoing, target, phase):
        g, o = places[chunk]
        axis_all(chunk, incoming, phase).wait_recv()
        sub = SUBS[chunk]
        for tile in range(TILES[chunk]):
            columns = slice(tile * 128, tile * 128 + 128)
            total = incoming[chunk][0, :, columns].astype(F32)
            for slot in range(1, 4):
                total = total + incoming[chunk][slot, :, columns].astype(F32)
            for row in range(ROWS_DEV):
                lanes[chunk][pl.ds(row * sub + tile, 16, stride=2 * sub), :] = total[
                    row * 16 : row * 16 + 16
                ]
        outgoing[chunk][...] = lanes[chunk][...].reshape(16, 2 * sub, 128).astype(BF16)
        start_plane(chunk, lambda to: outgoing[chunk].at[to], target, phase)
        target[chunk][o] = outgoing[chunk][o]

    def reduce_plane(chunk, target, phase):
        plane_all(chunk, target, phase).wait_recv()
        return jnp.sum(target[chunk][...].astype(F32), axis=0)

    def send_sums(chunk):
        heads = heads_by_axis[axes[chunk].kind]
        columns = columns_of(chunk)
        product = jnp.dot(
            heads[:, 0:128], op_buf[0, :, columns], preferred_element_type=F32
        ) + jnp.dot(heads[:, 128:256], op_buf[1, :, columns], preferred_element_type=F32)
        sums_out[chunk][...] = product.astype(BF16).reshape(sums_out[chunk].shape)
        start_reduce(chunk, sums_out, sums_in, 0)

    def add_sums(chunk):
        reduce_axis(chunk, sums_in, plane_out, plane_in, 0)

    square = [jnp.zeros((1, 1), F32) for row in range(ROWS_DEV)]

    def send_rows(chunk):
        resid = hidden_buf[chunk][...] + reduce_plane(chunk, plane_in, 0)
        resid_buf[chunk][...] = resid
        gather_out[chunk][...] = (resid * gain_buf[chunk][...]).astype(BF16)
        start_plane(chunk, lambda to: gather_out[chunk], gather_in, 1)
        gather_in[chunk][places[chunk][1]] = gather_out[chunk][...]
        for row in range(ROWS_DEV):
            piece = resid[row * SUBS[chunk] : row * SUBS[chunk] + SUBS[chunk]]
            square[row] = square[row] + jnp.sum(piece * piece, keepdims=True)

    def send_routes():
        lane = iota(1, (1, 128))
        tile_rows = iota(0, (16, 128))
        tile = jnp.zeros((16, 128), F32)
        for row in range(ROWS_DEV):
            dense = jnp.zeros((1, 128), F32)
            for slot in range(8):
                dense = dense + jnp.where(
                    lane % EXPERTS == ids_ref[row, slot], route_ref[row, slot], 0.0
                )
            factor = lax.rsqrt(square[row] / 7168.0 + 1e-06)
            dense = jnp.where(lane < 48, dense, jnp.broadcast_to(factor, (1, 128)))
            high, middle, low = three_terms(dense)
            line = jnp.where(
                (lane < 16) | (lane == 48),
                high,
                jnp.where(
                    (lane < 32) | (lane == 49),
                    middle,
                    jnp.where((lane < 48) | (lane == 50), low, 0.0),
                ),
            )
            tile = jnp.where(tile_rows == row * SUBS[CHUNKS], line, tile)
        gather_out[CHUNKS][...] = tile.astype(BF16)
        start_plane(CHUNKS, lambda to: gather_out[CHUNKS], gather_in, 1)
        gather_in[CHUNKS][places[CHUNKS][1]] = gather_out[CHUNKS][...]

    def spread_rows(chunk):
        g, o = places[chunk]
        plane_all(chunk, gather_in, 1).wait_recv()
        sub = SUBS[chunk]
        lanes[chunk][...] = gather_in[chunk][...].reshape(32 * sub, 128).astype(F32)
        for tile in range(TILES[chunk]):
            for row in range(ROWS_DEV):
                rows_in[chunk][
                    g, row * 16 : row * 16 + 16, tile * 128 : tile * 128 + 128
                ] = lanes[chunk][pl.ds(row * sub + tile, 16, stride=2 * sub), :].astype(BF16)
        for step in (2, 1, 3):
            axis_copy(
                chunk, rows_in[chunk].at[g], rows_in[chunk].at[g], 1, lax.rem(g + step, 4)
            ).start()

    gate = [jnp.zeros((128, 256), F32) for piece in range(2)]
    upper = [jnp.zeros((128, 256), F32) for piece in range(2)]

    def common_order(chunk, block):
        return jnp.dot(
            one_hot(rows_i, axes[chunk].key(cols_i)), block, preferred_element_type=F32
        ).astype(BF16)

    def expert_in(chunk):
        axis_all(chunk, rows_in, 1).wait_recv()
        block = common_order(chunk, rows_in[chunk][...].reshape(128, TILES[chunk] * 128))
        depth = columns_of(chunk)
        for piece in range(2):
            gate[piece] = gate[piece] + jnp.dot(
                block, wg_buf[piece, depth, :], preferred_element_type=F32
            )
            upper[piece] = upper[piece] + jnp.dot(
                block, wu_buf[piece, depth, :], preferred_element_type=F32
            )

    def each(step, wave):
        for chunk in WAVES[wave]:
            step(chunk)

    each(send_sums, 0)
    each(send_sums, 1)
    each(add_sums, 0)
    each(add_sums, 1)
    each(send_rows, 0)
    each(send_rows, 1)
    send_routes()
    each(spread_rows, 0)
    each(spread_rows, 1)
    spread_rows(CHUNKS)
    for index in range(2, 5):
        loads[index].wait()
        swaps[index].wait_recv()
    each(expert_in, 0)
    each(expert_in, 1)

    axis_all(CHUNKS, rows_in, 1).wait_recv()
    named = common_order(CHUNKS, rows_in[CHUNKS][...].reshape(128, 128))
    factor = jnp.sum(
        jnp.where((cols_i >= 48) & (cols_i < 51), named.astype(F32), 0.0), axis=1, keepdims=True
    )
    rows_all[:, 512:640] = named
    for piece in range(2):
        value = factor * gate[piece]
        rows_all[:, piece * 256 : piece * 256 + 256] = (
            value / (1.0 + jnp.exp(-value)) * (factor * upper[piece])
        ).astype(BF16)
    for kind in range(3):
        hidden_units = jnp.dot(
            one_hot(Axis(kind).key(rows_i), cols_i), rows_all[...], preferred_element_type=F32
        )
        units_by_axis[kind] = hidden_units[:, 0:512].astype(BF16)
        for piece in range(2):
            expert = piece * 8 + me // 8
            mine = (cols_i < 48) & (cols_i % EXPERTS == expert)
            weight = jnp.sum(
                jnp.where(mine, hidden_units[:, 512:640], 0.0), axis=1, keepdims=True
            )
            weight_by_axis[kind, piece] = jnp.broadcast_to(weight, (128, 128))

    def send_back(chunk):
        units = units_by_axis[axes[chunk].kind]
        columns = columns_of(chunk)
        product = jnp.zeros((128, TILES[chunk] * 128), F32)
        for piece in range(2):
            weight = weight_by_axis[axes[chunk].kind, piece]
            product = product + jnp.concatenate([weight] * TILES[chunk], axis=1) * jnp.dot(
                units[:, piece * 256 : piece * 256 + 256],
                wd_buf[piece, :, columns],
                preferred_element_type=F32,
            )
        back_out[chunk][...] = product.astype(BF16).reshape(back_out[chunk].shape)
        start_reduce(chunk, back_out, back_in, 2)

    def add_back(chunk):
        reduce_axis(chunk, back_in, plane_out2, plane_in2, 2)

    def finish(chunk):
        total = resid_buf[chunk][...] + reduce_plane(chunk, plane_in2, 2)
        for tile in range(TILES[chunk]):
            column = (FIRST[chunk] + tile) * 128
            for row in range(ROWS_DEV):
                at = row * SUBS[chunk] + tile
                out_ref[row : row + 1, column : column + 128] = total[at : at + 1, :]

    each(send_back, 0)
    each(send_back, 1)
    each(add_back, 0)
    each(add_back, 1)
    each(finish, 0)
    each(finish, 1)

    for swap in swaps:
        swap.wait_send()
    a2a_all.wait_send()
    for chunk in range(CHUNKS):
        axis_all(chunk, sums_in, 0).wait_send()
        axis_all(chunk, rows_in, 1).wait_send()
        axis_all(chunk, back_in, 2).wait_send()
        for phase, target in enumerate((plane_in, gather_in, plane_in2)):
            plane_all(chunk, target, phase).wait_send()
    axis_all(CHUNKS, rows_in, 1).wait_send()
    plane_all(CHUNKS, gather_in, 1).wait_send()


def layer(lengths, queries, cache, hidden_in, expert_ids, route_weights, norm_gain, value_up, out_proj, w_gate, w_up, w_down):
    vmem = pl.BlockSpec(memory_space=pltpu.VMEM)
    smem = pl.BlockSpec(memory_space=pltpu.SMEM)
    hbm = pl.BlockSpec(memory_space=pl.ANY)
    dma = pltpu.SemaphoreType.DMA
    wides = [tiles * 128 for tiles in TILES]
    return pl.pallas_call(
        layer_kernel,
        out_shape=jax.ShapeDtypeStruct((2, 7168), F32),
        in_specs=[smem, hbm, hbm, hbm, smem, smem, hbm, hbm, hbm, hbm, hbm, hbm],
        out_specs=vmem,
        scratch_shapes=[
            pltpu.VMEM((2, 576, 128), BF16),
            pltpu.VMEM((2, 7168), BF16),
            pltpu.VMEM((1, 7168), F32),
            pltpu.VMEM((2, 576, 2048), BF16),
            pltpu.VMEM((128, 2048), F32),
            pltpu.VMEM((128, 2048), BF16),
            pltpu.VMEM((2, 512, 128), BF16),
            pltpu.VMEM((2, 128, 7168), BF16),
            pltpu.VMEM((2, 7168, 256), BF16),
            pltpu.VMEM((2, 7168, 256), BF16),
            pltpu.VMEM((2, 256, 7168), BF16),
            pltpu.VMEM((64, 16, 128), BF16),
            pltpu.VMEM((64, 16, 128), BF16),
            pltpu.VMEM((1024, 128), F32),
            pltpu.VMEM((128, 256), BF16),
            [pltpu.VMEM((4, 32, wide), BF16) for wide in wides],
            [pltpu.VMEM((4, 32, wide), BF16) for wide in wides],
            [pltpu.VMEM((32 * sub, 128), F32) for sub in SUBS],
            [pltpu.VMEM((16, 2 * sub, 128), BF16) for sub in SUBS],
            [pltpu.VMEM((16, 2 * sub, 128), BF16) for sub in SUBS],
            [pltpu.VMEM((2 * sub, 128), F32) for sub in SUBS],
            [pltpu.VMEM((2 * sub, 128), F32) for sub in SUBS],
            [pltpu.VMEM((2 * sub, 128), F32) for sub in SUBS],
            [pltpu.VMEM((16, 2 * sub, 128), BF16) for sub in SUBS],
            [pltpu.VMEM((2 * sub, 128), BF16) for sub in SUBS],
            [pltpu.VMEM((4, 32, wide), BF16) for wide in wides],
            pltpu.VMEM((128, 640), BF16),
            pltpu.VMEM((3, 128, 256), BF16),
            pltpu.VMEM((3, 128, 512), BF16),
            pltpu.VMEM((3, 2, 128, 128), F32),
            [pltpu.VMEM((4, 32, wide), BF16) for wide in wides],
            [pltpu.VMEM((4, 32, wide), BF16) for wide in wides],
            [pltpu.VMEM((16, 2 * sub, 128), BF16) for sub in SUBS],
            [pltpu.VMEM((16, 2 * sub, 128), BF16) for sub in SUBS],
            dma((3,)),
            dma((2, 4)),
            dma((5,)),
            dma((5,)),
            dma((5,)),
            dma,
            dma,
            dma((3, CHUNKS + 1)),
            dma((3, CHUNKS + 1)),
            dma((3, CHUNKS + 1)),
            dma((3, CHUNKS + 1)),
        ],
        compiler_params=pltpu.CompilerParams(
            collective_id=0, has_side_effects=True, vmem_limit_bytes=58 * MIB
        ),
        name="layer",
    )(
        lengths,
        queries,
        cache,
        hidden_in,
        expert_ids,
        route_weights,
        norm_gain.reshape(1, -1),
        value_up.reshape(512, 128),
        out_proj,
        w_gate,
        w_up,
        w_down,
    )


def per_device(
    hidden_in,
    queries,
    latent_cache,
    cache_lengths,
    value_up,
    out_proj,
    norm_gain,
    expert_ids,
    route_weights,
    w_gate,
    w_up,
    w_down,
):
    out = layer(
        cache_lengths,
        queries.transpose(0, 2, 1),
        latent_cache.transpose(0, 2, 1),
        hidden_in,
        expert_ids,
        route_weights,
        norm_gain,
        value_up,
        out_proj,
        w_gate,
        w_up,
        w_down,
    )
    return out.astype(BF16)


def solution(mesh):
    rows = P(("sec", "dev"), None)
    rows3 = P(("sec", "dev"), None, None)
    placed = (
        rows,
        rows3,
        rows3,
        P(("sec", "dev")),
        rows3,
        rows,
        P(),
        rows,
        rows,
        P(None, ("sec", "dev")),
        P(None, ("sec", "dev")),
        rows,
    )
    return jax.shard_map(
        per_device, mesh=mesh, in_specs=placed, out_specs=rows, check_vma=False
    )
```

```python
import jax
import jax.numpy as jnp
from jax import lax
from jax.experimental import pallas as pl
from jax.experimental.pallas import tpu as pltpu
from jax.sharding import PartitionSpec as P

EXPERTS = 16
ROWS_DEV = 2
MESH = pl.DeviceIdType.MESH
F32 = jnp.float32
BF16 = jnp.bfloat16
MIB = 2**20

score_scale = 0.07216878364870322

TILES = (11, 11, 10, 8, 8, 8, 1)
SUBS = (16, 16, 16, 8, 8, 8, 8)
FIRST = (0, 11, 22, 32, 40, 48)
CHUNKS = 6
WAVES = ((0, 1, 2), (3, 4, 5))
RING = (0, 1, 2, 1)
FAR_FIRST = sorted(
    [(x, z, y) for x in range(4) for z in range(4) for y in range(4)][1:],
    key=lambda at: -RING[at[0]] - RING[at[1]] - RING[at[2]],
)


def columns_of(chunk):
    return slice(FIRST[chunk] * 128, (FIRST[chunk] + TILES[chunk]) * 128)


class Axis:
    def __init__(self, kind):
        self.kind = kind
        self.first = (16, 4, 1)[kind]
        self.high = (4, 16, 16)[kind]
        self.low = (1, 1, 4)[kind]

    def dev(self, g, o):
        return g * self.first + (o // 4) * self.high + (o % 4) * self.low

    def place(self, dev):
        return (dev // self.first) % 4, (dev // self.high) % 4 * 4 + (dev // self.low) % 4

    def key(self, q):
        return ((q // 16) % 2) * 64 + self.dev(q // 32, q % 16)


def one_hot(rows_key, cols_key):
    return jnp.where(rows_key == cols_key, 1.0, 0.0).astype(BF16)


def iota(axis, shape=(128, 128)):
    return lax.broadcasted_iota(jnp.int32, shape, axis)


def three_terms(value):
    high = value.astype(BF16).astype(F32)
    middle = (value - high).astype(BF16).astype(F32)
    return high, middle, value - high - middle


def layer_kernel(
    lengths_ref,
    queries_ref,
    cache_ref,
    hidden_ref,
    ids_ref,
    route_ref,
    gain_ref,
    value_up_ref,
    out_proj_ref,
    w_gate_ref,
    w_up_ref,
    w_down_ref,
    out_ref,
    query_buf,
    hidden_rows,
    gain_row,
    cache_buf,
    score_buf,
    weight_buf,
    vu_buf,
    op_buf,
    wg_buf,
    wu_buf,
    wd_buf,
    msg_buf,
    by_head,
    spread,
    heads_buf,
    sums_out,
    sums_in,
    lanes,
    plane_out,
    plane_in,
    resid_buf,
    hidden_buf,
    gain_buf,
    gather_in,
    gather_out,
    rows_in,
    rows_all,
    to_axis,
    from_axis,
    heads_by_axis,
    units_by_axis,
    weight_by_axis,
    back_out,
    back_in,
    plane_out2,
    plane_in2,
    small_sem,
    cache_sem,
    load_sem,
    swap_send,
    swap_recv,
    a2a_send,
    a2a_recv,
    axis_send,
    axis_recv,
    plane_send,
    plane_recv,
):
    sec = lax.axis_index("sec")
    me = lax.axis_index("dev")
    axes = [Axis(kind) for kind in (0, 1, 2, 0, 1, 2, 2)]
    places = [axis.place(me) for axis in axes]

    barrier = pltpu.get_barrier_semaphore()

    def greet_all():
        for step in range(1, 64):
            pl.semaphore_signal(
                barrier, inc=1, device_id=(sec, lax.rem(me + step, 64)), device_id_type=MESH
            )
        pl.semaphore_signal(barrier, inc=1, device_id=(1 - sec, me), device_id_type=MESH)

    weights = (
        (value_up_ref, vu_buf),
        (out_proj_ref, op_buf),
        (w_gate_ref, wg_buf),
        (w_up_ref, wu_buf),
        (w_down_ref, wd_buf),
    )
    loads = [
        pltpu.make_async_copy(source, target.at[sec], load_sem.at[index])
        for index, (source, target) in enumerate(weights)
    ]
    swaps = [
        pltpu.make_async_remote_copy(
            source,
            target.at[sec],
            swap_send.at[index],
            swap_recv.at[index],
            device_id=(1 - sec, me),
            device_id_type=MESH,
        )
        for index, (source, target) in enumerate(weights)
    ]
    cache_loads = [
        pltpu.make_async_copy(cache_ref.at[row], cache_buf.at[row], cache_sem.at[row])
        for row in range(ROWS_DEV)
    ]
    small_loads = [
        pltpu.make_async_copy(source, target, small_sem.at[index])
        for index, (source, target) in enumerate(
            ((queries_ref, query_buf), (hidden_ref, hidden_rows), (gain_ref, gain_row))
        )
    ]
    for copy in [small_loads[0]] + cache_loads + small_loads[1:]:
        copy.start()
    greet_all()
    small_loads[0].wait()
    cache_loads[0].wait()
    cache_loads[1].wait()
    for load in loads:
        load.start()

    span, step_len = cache_ref.shape[2], 512
    for row in range(ROWS_DEV):
        length = lengths_ref[row]
        query = query_buf[row].T
        peak = jnp.full((128, 1), -1e30, F32)
        for start in range(0, span, step_len):
            score = jnp.dot(
                query, cache_buf[row, :, start : start + step_len], preferred_element_type=F32
            )
            position = start + iota(1, (1, step_len))
            score = jnp.where(position < length, score * score_scale, -1e30)
            score_buf[row, :, start : start + step_len] = score
            peak = jnp.maximum(peak, jnp.max(score, axis=1, keepdims=True))
        total = jnp.zeros((128, 1), F32)
        for start in range(0, span, step_len):
            weight = jnp.exp(score_buf[row, :, start : start + step_len] - peak)
            total = total + jnp.sum(weight, axis=1, keepdims=True)
            weight_buf[row, :, start : start + step_len] = weight.astype(BF16)
        summed = lax.dot_general(
            cache_buf[row, 0:512, :],
            weight_buf[row],
            (((1,), (1,)), ((), ())),
            preferred_element_type=F32,
        )
        attended = summed.T / total
        for half in range(2):
            for chunk in range(4):
                spread[pl.ds(row * 8 + half * 4 + chunk, 64, stride=16), :] = attended[
                    half * 64 : half * 64 + 64, chunk * 128 : chunk * 128 + 128
                ]
    pl.semaphore_wait(barrier, 64)
    swaps[0].start()
    swaps[1].start()
    msg_buf[...] = spread[...].astype(BF16).reshape(64, 16, 128)

    for x, z, y in FAR_FIRST:
        peer = (me // 16 + x) % 4 * 16 + (me // 4 % 4 + z) % 4 * 4 + (me + y) % 4
        pltpu.make_async_remote_copy(
            msg_buf.at[peer],
            by_head.at[me],
            a2a_send,
            a2a_recv,
            device_id=(sec, peer),
            device_id_type=MESH,
        ).start()
    for swap in swaps[2:]:
        swap.start()
    by_head[me] = msg_buf[me]

    rows_i, cols_i = iota(0), iota(1)
    for kind in range(3):
        to_axis[kind] = one_hot(Axis(kind).key(rows_i), cols_i)
        from_axis[kind] = one_hot(rows_i, Axis(kind).key(cols_i))
    small_loads[1].wait()
    small_loads[2].wait()
    hidden = hidden_rows[...].astype(F32)
    gains = gain_row[...]
    for chunk in range(CHUNKS):
        hidden_buf[chunk][...] = jnp.zeros(hidden_buf[chunk].shape, F32)
        gain_buf[chunk][...] = jnp.zeros(gain_buf[chunk].shape, F32)
        lanes[chunk][...] = jnp.zeros(lanes[chunk].shape, F32)
        for tile in range(TILES[chunk]):
            column = (FIRST[chunk] + tile) * 128
            for row in range(ROWS_DEV):
                at = row * SUBS[chunk] + tile
                hidden_buf[chunk][at : at + 1, :] = hidden[row : row + 1, column : column + 128]
                gain_buf[chunk][at : at + 1, :] = gains[:, column : column + 128]

    a2a_all = pltpu.make_async_remote_copy(
        msg_buf.at[pl.ds(0, 63)],
        by_head.at[pl.ds(0, 63)],
        a2a_send,
        a2a_recv,
        device_id=(sec, lax.rem(me + 1, 64)),
        device_id_type=MESH,
    )
    loads[0].wait()
    loads[1].wait()
    swaps[0].wait_recv()
    swaps[1].wait_recv()
    a2a_all.wait_recv()

    spread[...] = by_head[...].reshape(1024, 128).astype(F32)
    for half in range(2):
        parts = []
        for row in range(ROWS_DEV):
            parts.append(
                jnp.concatenate(
                    [
                        spread[pl.ds(row * 8 + half * 4 + chunk, 64, stride=16), :].astype(BF16)
                        for chunk in range(4)
                    ],
                    axis=1,
                )
            )
        heads_buf[:, half * 128 : half * 128 + 128] = jnp.dot(
            jnp.concatenate(parts), vu_buf[half], preferred_element_type=F32
        ).astype(BF16)

    for kind in range(3):
        heads_by_axis[kind] = jnp.dot(
            to_axis[kind], heads_buf[...], preferred_element_type=F32
        ).astype(BF16)

    def axis_copy(chunk, source, target, phase, to):
        axis = axes[chunk]
        return pltpu.make_async_remote_copy(
            source,
            target,
            axis_send.at[phase, chunk],
            axis_recv.at[phase, chunk],
            device_id=(sec, axis.dev(to, places[chunk][1])),
            device_id_type=MESH,
        )

    def axis_all(chunk, target, phase):
        whole = target[chunk].at[pl.ds(0, 3)]
        return axis_copy(chunk, whole, whole, phase, lax.rem(places[chunk][0] + 1, 4))

    def start_reduce(chunk, outgoing, incoming, phase):
        g, o = places[chunk]
        for step in (2, 1, 3):
            to = lax.rem(g + step, 4)
            axis_copy(
                chunk, outgoing[chunk].at[to], incoming[chunk].at[g], phase, to
            ).start()
        incoming[chunk][g] = outgoing[chunk][g]

    def plane_copy(chunk, source, target, phase, to):
        return pltpu.make_async_remote_copy(
            source,
            target,
            plane_send.at[phase, chunk],
            plane_recv.at[phase, chunk],
            device_id=(sec, axes[chunk].dev(places[chunk][0], to)),
            device_id_type=MESH,
        )

    def plane_all(chunk, target, phase):
        whole = target[chunk].at[pl.ds(0, 15)]
        return plane_copy(chunk, whole, whole, phase, lax.rem(places[chunk][1] + 1, 16))

    def start_plane(chunk, source_of, target, phase):
        g, o = places[chunk]

        for x, high, low in FAR_FIRST:
            if x == 0:
                to = (o // 4 + high) % 4 * 4 + (o + low) % 4
                plane_copy(chunk, source_of(to), target[chunk].at[o], phase, to).start()

    def reduce_axis(chunk, incoming, outgoing, target, phase):
        g, o = places[chunk]
        axis_all(chunk, incoming, phase).wait_recv()
        sub = SUBS[chunk]
        for tile in range(TILES[chunk]):
            columns = slice(tile * 128, tile * 128 + 128)
            total = incoming[chunk][0, :, columns].astype(F32)
            for slot in range(1, 4):
                total = total + incoming[chunk][slot, :, columns].astype(F32)
            for row in range(ROWS_DEV):
                lanes[chunk][pl.ds(row * sub + tile, 16, stride=2 * sub), :] = total[
                    row * 16 : row * 16 + 16
                ]
        outgoing[chunk][...] = lanes[chunk][...].reshape(16, 2 * sub, 128).astype(BF16)
        start_plane(chunk, lambda to: outgoing[chunk].at[to], target, phase)
        target[chunk][o] = outgoing[chunk][o]

    def reduce_plane(chunk, target, phase):
        plane_all(chunk, target, phase).wait_recv()
        return jnp.sum(target[chunk][...].astype(F32), axis=0)

    def send_sums(chunk):
        heads = heads_by_axis[axes[chunk].kind]
        columns = columns_of(chunk)
        product = jnp.dot(
            heads[:, 0:128], op_buf[0, :, columns], preferred_element_type=F32
        ) + jnp.dot(heads[:, 128:256], op_buf[1, :, columns], preferred_element_type=F32)
        sums_out[chunk][...] = product.astype(BF16).reshape(sums_out[chunk].shape)
        start_reduce(chunk, sums_out, sums_in, 0)

    def add_sums(chunk):
        reduce_axis(chunk, sums_in, plane_out, plane_in, 0)

    square = [jnp.zeros((1, 1), F32) for row in range(ROWS_DEV)]

    def send_rows(chunk):
        resid = hidden_buf[chunk][...] + reduce_plane(chunk, plane_in, 0)
        resid_buf[chunk][...] = resid
        gather_out[chunk][...] = (resid * gain_buf[chunk][...]).astype(BF16)
        start_plane(chunk, lambda to: gather_out[chunk], gather_in, 1)
        gather_in[chunk][places[chunk][1]] = gather_out[chunk][...]
        for row in range(ROWS_DEV):
            piece = resid[row * SUBS[chunk] : row * SUBS[chunk] + SUBS[chunk]]
            square[row] = square[row] + jnp.sum(piece * piece, keepdims=True)

    def send_routes():
        lane = iota(1, (1, 128))
        tile_rows = iota(0, (16, 128))
        tile = jnp.zeros((16, 128), F32)
        for row in range(ROWS_DEV):
            dense = jnp.zeros((1, 128), F32)
            for slot in range(8):
                dense = dense + jnp.where(
                    lane % EXPERTS == ids_ref[row, slot], route_ref[row, slot], 0.0
                )
            factor = lax.rsqrt(square[row] / 7168.0 + 1e-06)
            dense = jnp.where(lane < 48, dense, jnp.broadcast_to(factor, (1, 128)))
            high, middle, low = three_terms(dense)
            line = jnp.where(
                (lane < 16) | (lane == 48),
                high,
                jnp.where(
                    (lane < 32) | (lane == 49),
                    middle,
                    jnp.where((lane < 48) | (lane == 50), low, 0.0),
                ),
            )
            tile = jnp.where(tile_rows == row * SUBS[CHUNKS], line, tile)
        gather_out[CHUNKS][...] = tile.astype(BF16)
        start_plane(CHUNKS, lambda to: gather_out[CHUNKS], gather_in, 1)
        gather_in[CHUNKS][places[CHUNKS][1]] = gather_out[CHUNKS][...]

    def spread_rows(chunk):
        g, o = places[chunk]
        plane_all(chunk, gather_in, 1).wait_recv()
        sub = SUBS[chunk]
        lanes[chunk][...] = gather_in[chunk][...].reshape(32 * sub, 128).astype(F32)
        for tile in range(TILES[chunk]):
            for row in range(ROWS_DEV):
                rows_in[chunk][
                    g, row * 16 : row * 16 + 16, tile * 128 : tile * 128 + 128
                ] = lanes[chunk][pl.ds(row * sub + tile, 16, stride=2 * sub), :].astype(BF16)
        for step in (2, 1, 3):
            axis_copy(
                chunk, rows_in[chunk].at[g], rows_in[chunk].at[g], 1, lax.rem(g + step, 4)
            ).start()

    gate = [jnp.zeros((128, 256), F32) for piece in range(2)]
    upper = [jnp.zeros((128, 256), F32) for piece in range(2)]

    def common_order(chunk, block):
        return jnp.dot(
            from_axis[axes[chunk].kind], block, preferred_element_type=F32
        ).astype(BF16)

    def expert_in(chunk):
        axis_all(chunk, rows_in, 1).wait_recv()
        block = common_order(chunk, rows_in[chunk][...].reshape(128, TILES[chunk] * 128))
        depth = columns_of(chunk)
        for piece in range(2):
            gate[piece] = gate[piece] + jnp.dot(
                block, wg_buf[piece, depth, :], preferred_element_type=F32
            )
            upper[piece] = upper[piece] + jnp.dot(
                block, wu_buf[piece, depth, :], preferred_element_type=F32
            )

    def each(step, wave):
        for chunk in WAVES[wave]:
            step(chunk)

    each(send_sums, 0)
    each(send_sums, 1)
    each(add_sums, 0)
    each(add_sums, 1)
    each(send_rows, 0)
    each(send_rows, 1)
    send_routes()
    each(spread_rows, 0)
    each(spread_rows, 1)
    spread_rows(CHUNKS)
    for index in range(2, 5):
        loads[index].wait()
        swaps[index].wait_recv()
    each(expert_in, 0)
    each(expert_in, 1)

    axis_all(CHUNKS, rows_in, 1).wait_recv()
    named = common_order(CHUNKS, rows_in[CHUNKS][...].reshape(128, 128))
    factor = jnp.sum(
        jnp.where((cols_i >= 48) & (cols_i < 51), named.astype(F32), 0.0), axis=1, keepdims=True
    )
    rows_all[:, 512:640] = named
    for piece in range(2):
        value = factor * gate[piece]
        rows_all[:, piece * 256 : piece * 256 + 256] = (
            value / (1.0 + jnp.exp(-value)) * (factor * upper[piece])
        ).astype(BF16)
    for kind in range(3):
        hidden_units = jnp.dot(to_axis[kind], rows_all[...], preferred_element_type=F32)
        units_by_axis[kind] = hidden_units[:, 0:512].astype(BF16)
        for piece in range(2):
            expert = piece * 8 + me // 8
            mine = (cols_i < 48) & (cols_i % EXPERTS == expert)
            weight = jnp.sum(
                jnp.where(mine, hidden_units[:, 512:640], 0.0), axis=1, keepdims=True
            )
            weight_by_axis[kind, piece] = jnp.broadcast_to(weight, (128, 128))

    def send_back(chunk):
        units = units_by_axis[axes[chunk].kind]
        columns = columns_of(chunk)
        product = jnp.zeros((128, TILES[chunk] * 128), F32)
        for piece in range(2):
            weight = weight_by_axis[axes[chunk].kind, piece]
            product = product + jnp.concatenate([weight] * TILES[chunk], axis=1) * jnp.dot(
                units[:, piece * 256 : piece * 256 + 256],
                wd_buf[piece, :, columns],
                preferred_element_type=F32,
            )
        back_out[chunk][...] = product.astype(BF16).reshape(back_out[chunk].shape)
        start_reduce(chunk, back_out, back_in, 2)

    def add_back(chunk):
        reduce_axis(chunk, back_in, plane_out2, plane_in2, 2)

    def finish(chunk):
        total = resid_buf[chunk][...] + reduce_plane(chunk, plane_in2, 2)
        for tile in range(TILES[chunk]):
            column = (FIRST[chunk] + tile) * 128
            for row in range(ROWS_DEV):
                at = row * SUBS[chunk] + tile
                out_ref[row : row + 1, column : column + 128] = total[at : at + 1, :]

    each(send_back, 0)
    each(send_back, 1)
    each(add_back, 0)
    each(add_back, 1)
    each(finish, 0)
    each(finish, 1)

    for swap in swaps:
        swap.wait_send()
    a2a_all.wait_send()
    for chunk in range(CHUNKS):
        axis_all(chunk, sums_in, 0).wait_send()
        axis_all(chunk, rows_in, 1).wait_send()
        axis_all(chunk, back_in, 2).wait_send()
        for phase, target in enumerate((plane_in, gather_in, plane_in2)):
            plane_all(chunk, target, phase).wait_send()
    axis_all(CHUNKS, rows_in, 1).wait_send()
    plane_all(CHUNKS, gather_in, 1).wait_send()


def layer(lengths, queries, cache, hidden_in, expert_ids, route_weights, norm_gain, value_up, out_proj, w_gate, w_up, w_down):
    vmem = pl.BlockSpec(memory_space=pltpu.VMEM)
    smem = pl.BlockSpec(memory_space=pltpu.SMEM)
    hbm = pl.BlockSpec(memory_space=pl.ANY)
    dma = pltpu.SemaphoreType.DMA
    wides = [tiles * 128 for tiles in TILES]
    return pl.pallas_call(
        layer_kernel,
        out_shape=jax.ShapeDtypeStruct((2, 7168), F32),
        in_specs=[smem, hbm, hbm, hbm, smem, smem, hbm, hbm, hbm, hbm, hbm, hbm],
        out_specs=vmem,
        scratch_shapes=[
            pltpu.VMEM((2, 576, 128), BF16),
            pltpu.VMEM((2, 7168), BF16),
            pltpu.VMEM((1, 7168), F32),
            pltpu.VMEM((2, 576, 2048), BF16),
            pltpu.VMEM((2, 128, 2048), F32),
            pltpu.VMEM((2, 128, 2048), BF16),
            pltpu.VMEM((2, 512, 128), BF16),
            pltpu.VMEM((2, 128, 7168), BF16),
            pltpu.VMEM((2, 7168, 256), BF16),
            pltpu.VMEM((2, 7168, 256), BF16),
            pltpu.VMEM((2, 256, 7168), BF16),
            pltpu.VMEM((64, 16, 128), BF16),
            pltpu.VMEM((64, 16, 128), BF16),
            pltpu.VMEM((1024, 128), F32),
            pltpu.VMEM((128, 256), BF16),
            [pltpu.VMEM((4, 32, wide), BF16) for wide in wides],
            [pltpu.VMEM((4, 32, wide), BF16) for wide in wides],
            [pltpu.VMEM((32 * sub, 128), F32) for sub in SUBS],
            [pltpu.VMEM((16, 2 * sub, 128), BF16) for sub in SUBS],
            [pltpu.VMEM((16, 2 * sub, 128), BF16) for sub in SUBS],
            [pltpu.VMEM((2 * sub, 128), F32) for sub in SUBS],
            [pltpu.VMEM((2 * sub, 128), F32) for sub in SUBS],
            [pltpu.VMEM((2 * sub, 128), F32) for sub in SUBS],
            [pltpu.VMEM((16, 2 * sub, 128), BF16) for sub in SUBS],
            [pltpu.VMEM((2 * sub, 128), BF16) for sub in SUBS],
            [pltpu.VMEM((4, 32, wide), BF16) for wide in wides],
            pltpu.VMEM((128, 640), BF16),
            pltpu.VMEM((3, 128, 128), BF16),
            pltpu.VMEM((3, 128, 128), BF16),
            pltpu.VMEM((3, 128, 256), BF16),
            pltpu.VMEM((3, 128, 512), BF16),
            pltpu.VMEM((3, 2, 128, 128), F32),
            [pltpu.VMEM((4, 32, wide), BF16) for wide in wides],
            [pltpu.VMEM((4, 32, wide), BF16) for wide in wides],
            [pltpu.VMEM((16, 2 * sub, 128), BF16) for sub in SUBS],
            [pltpu.VMEM((16, 2 * sub, 128), BF16) for sub in SUBS],
            dma((3,)),
            dma((2,)),
            dma((5,)),
            dma((5,)),
            dma((5,)),
            dma,
            dma,
            dma((3, CHUNKS + 1)),
            dma((3, CHUNKS + 1)),
            dma((3, CHUNKS + 1)),
            dma((3, CHUNKS + 1)),
        ],
        compiler_params=pltpu.CompilerParams(
            collective_id=0, has_side_effects=True, vmem_limit_bytes=58 * MIB
        ),
        name="layer",
    )(
        lengths,
        queries,
        cache,
        hidden_in,
        expert_ids,
        route_weights,
        norm_gain.reshape(1, -1),
        value_up.reshape(512, 128),
        out_proj,
        w_gate,
        w_up,
        w_down,
    )


def per_device(
    hidden_in,
    queries,
    latent_cache,
    cache_lengths,
    value_up,
    out_proj,
    norm_gain,
    expert_ids,
    route_weights,
    w_gate,
    w_up,
    w_down,
):
    out = layer(
        cache_lengths,
        queries.transpose(0, 2, 1),
        latent_cache.transpose(0, 2, 1),
        hidden_in,
        expert_ids,
        route_weights,
        norm_gain,
        value_up,
        out_proj,
        w_gate,
        w_up,
        w_down,
    )
    return out.astype(BF16)


def solution(mesh):
    rows = P(("sec", "dev"), None)
    rows3 = P(("sec", "dev"), None, None)
    placed = (
        rows,
        rows3,
        rows3,
        P(("sec", "dev")),
        rows3,
        rows,
        P(),
        rows,
        rows,
        P(None, ("sec", "dev")),
        P(None, ("sec", "dev")),
        rows,
    )
    return jax.shard_map(
        per_device, mesh=mesh, in_specs=placed, out_specs=rows, check_vma=False
    )
```

```python
import jax
import jax.numpy as jnp
from jax import lax
from jax.experimental import pallas as pl
from jax.experimental.pallas import tpu as pltpu
from jax.sharding import PartitionSpec as P

EXPERTS = 16
ROWS_DEV = 2
MESH = pl.DeviceIdType.MESH
F32 = jnp.float32
BF16 = jnp.bfloat16
MIB = 2**20

score_scale = 0.07216878364870322

TILES = (11, 11, 10, 8, 8, 8, 1)
SUBS = (16, 16, 16, 8, 8, 8, 8)
FIRST = (0, 11, 22, 32, 40, 48)
CHUNKS = 6
WAVES = ((0, 1, 2), (3, 4, 5))
RING = (0, 1, 2, 1)
FAR_FIRST = sorted(
    [(x, z, y) for x in range(4) for z in range(4) for y in range(4)][1:],
    key=lambda at: -RING[at[0]] - RING[at[1]] - RING[at[2]],
)


def columns_of(chunk):
    return slice(FIRST[chunk] * 128, (FIRST[chunk] + TILES[chunk]) * 128)


class Axis:
    def __init__(self, kind):
        self.kind = kind
        self.first = (16, 4, 1)[kind]
        self.high = (4, 16, 16)[kind]
        self.low = (1, 1, 4)[kind]

    def dev(self, g, o):
        return g * self.first + (o // 4) * self.high + (o % 4) * self.low

    def place(self, dev):
        return (dev // self.first) % 4, (dev // self.high) % 4 * 4 + (dev // self.low) % 4

    def key(self, q):
        return ((q // 16) % 2) * 64 + self.dev(q // 32, q % 16)


def one_hot(rows_key, cols_key):
    return jnp.where(rows_key == cols_key, 1.0, 0.0).astype(BF16)


def iota(axis, shape=(128, 128)):
    return lax.broadcasted_iota(jnp.int32, shape, axis)


def three_terms(value):
    high = value.astype(BF16).astype(F32)
    middle = (value - high).astype(BF16).astype(F32)
    return high, middle, value - high - middle


def layer_kernel(
    lengths_hbm,
    queries_ref,
    cache_ref,
    hidden_ref,
    ids_hbm,
    route_hbm,
    gain_ref,
    value_up_ref,
    out_proj_ref,
    w_gate_ref,
    w_up_ref,
    w_down_ref,
    out_ref,
    lengths_ref,
    ids_ref,
    route_ref,
    query_buf,
    hidden_rows,
    gain_row,
    cache_buf,
    score_buf,
    weight_buf,
    vu_buf,
    op_buf,
    wg_buf,
    wu_buf,
    wd_buf,
    msg_buf,
    by_head,
    spread,
    heads_buf,
    sums_out,
    sums_in,
    lanes,
    plane_out,
    plane_in,
    resid_buf,
    hidden_buf,
    gain_buf,
    gather_in,
    gather_out,
    rows_in,
    rows_all,
    to_axis,
    from_axis,
    back_axis,
    heads_by_axis,
    units_by_axis,
    weight_by_axis,
    back_out,
    back_in,
    plane_out2,
    plane_in2,
    small_sem,
    cache_sem,
    load_sem,
    swap_send,
    swap_recv,
    a2a_send,
    a2a_recv,
    axis_send,
    axis_recv,
    plane_send,
    plane_recv,
):
    sec = lax.axis_index("sec")
    me = lax.axis_index("dev")
    axes = [Axis(kind) for kind in (0, 1, 2, 0, 1, 2, 2)]
    places = [axis.place(me) for axis in axes]

    barrier = pltpu.get_barrier_semaphore()

    def greet_all():
        for step in range(1, 64):
            pl.semaphore_signal(
                barrier, inc=1, device_id=(sec, lax.rem(me + step, 64)), device_id_type=MESH
            )
        pl.semaphore_signal(barrier, inc=1, device_id=(1 - sec, me), device_id_type=MESH)

    weights = (
        (value_up_ref, vu_buf),
        (out_proj_ref, op_buf),
        (w_gate_ref, wg_buf),
        (w_up_ref, wu_buf),
        (w_down_ref, wd_buf),
    )
    loads = [
        pltpu.make_async_copy(source, target.at[sec], load_sem.at[index])
        for index, (source, target) in enumerate(weights)
    ]
    swaps = [
        pltpu.make_async_remote_copy(
            source,
            target.at[sec],
            swap_send.at[index],
            swap_recv.at[index],
            device_id=(1 - sec, me),
            device_id_type=MESH,
        )
        for index, (source, target) in enumerate(weights)
    ]
    cache_loads = []
    for row in range(ROWS_DEV):
        for piece in range(4):
            depth = pl.ds(piece * 144, 144)
            cache_loads.append(
                pltpu.make_async_copy(
                    cache_ref.at[row, depth, :],
                    cache_buf.at[row, depth, :],
                    cache_sem.at[row, piece],
                )
            )
    small_loads = [
        pltpu.make_async_copy(source, target, small_sem.at[index])
        for index, (source, target) in enumerate(
            (
                (queries_ref, query_buf),
                (hidden_ref, hidden_rows),
                (gain_ref, gain_row),
                (lengths_hbm, lengths_ref),
                (ids_hbm, ids_ref),
                (route_hbm, route_ref),
            )
        )
    ]
    for copy in [small_loads[0]] + cache_loads + small_loads[1:]:
        copy.start()
    greet_all()
    small_loads[0].wait()
    small_loads[3].wait()
    for load in cache_loads:
        load.wait()
    for load in loads:
        load.start()

    span, step_len = cache_ref.shape[2], 512
    for row in range(ROWS_DEV):
        length = lengths_ref[row]
        query = query_buf[row].T
        peak = jnp.full((128, 1), -1e30, F32)
        for start in range(0, span, step_len):
            score = jnp.dot(
                query, cache_buf[row, :, start : start + step_len], preferred_element_type=F32
            )
            position = start + iota(1, (1, step_len))
            score = jnp.where(position < length, score * score_scale, -1e30)
            score_buf[row, :, start : start + step_len] = score
            peak = jnp.maximum(peak, jnp.max(score, axis=1, keepdims=True))
        total = jnp.zeros((128, 1), F32)
        for start in range(0, span, step_len):
            weight = jnp.exp(score_buf[row, :, start : start + step_len] - peak)
            total = total + jnp.sum(weight, axis=1, keepdims=True)
            weight_buf[row, :, start : start + step_len] = weight.astype(BF16)
        summed = lax.dot_general(
            cache_buf[row, 0:512, :],
            weight_buf[row],
            (((1,), (1,)), ((), ())),
            preferred_element_type=F32,
        )
        attended = summed.T / total
        for half in range(2):
            for chunk in range(4):
                spread[pl.ds(row * 8 + half * 4 + chunk, 64, stride=16), :] = attended[
                    half * 64 : half * 64 + 64, chunk * 128 : chunk * 128 + 128
                ]
    pl.semaphore_wait(barrier, 64)
    swaps[0].start()
    swaps[1].start()
    msg_buf[...] = spread[...].astype(BF16).reshape(64, 16, 128)

    for x, z, y in FAR_FIRST:
        peer = (me // 16 + x) % 4 * 16 + (me // 4 % 4 + z) % 4 * 4 + (me + y) % 4
        pltpu.make_async_remote_copy(
            msg_buf.at[peer],
            by_head.at[me],
            a2a_send,
            a2a_recv,
            device_id=(sec, peer),
            device_id_type=MESH,
        ).start()
    by_head[me] = msg_buf[me]

    rows_i, cols_i = iota(0), iota(1)
    for kind in range(3):
        to_axis[kind] = one_hot(Axis(kind).key(rows_i), cols_i)
        from_axis[kind] = one_hot(Axis(0).key(rows_i), Axis(kind).key(cols_i))
        back_axis[kind] = one_hot(Axis(kind).key(rows_i), Axis(0).key(cols_i))
    for index in (1, 4, 5):
        small_loads[index].wait()
    small_loads[2].wait()
    hidden = hidden_rows[...].astype(F32)
    gains = gain_row[...]
    for chunk in range(CHUNKS):
        hidden_buf[chunk][...] = jnp.zeros(hidden_buf[chunk].shape, F32)
        gain_buf[chunk][...] = jnp.zeros(gain_buf[chunk].shape, F32)
        lanes[chunk][...] = jnp.zeros(lanes[chunk].shape, F32)
        for tile in range(TILES[chunk]):
            column = (FIRST[chunk] + tile) * 128
            for row in range(ROWS_DEV):
                at = row * SUBS[chunk] + tile
                hidden_buf[chunk][at : at + 1, :] = hidden[row : row + 1, column : column + 128]
                gain_buf[chunk][at : at + 1, :] = gains[:, column : column + 128]

    a2a_all = pltpu.make_async_remote_copy(
        msg_buf.at[pl.ds(0, 63)],
        by_head.at[pl.ds(0, 63)],
        a2a_send,
        a2a_recv,
        device_id=(sec, lax.rem(me + 1, 64)),
        device_id_type=MESH,
    )
    loads[0].wait()
    loads[1].wait()
    swaps[0].wait_recv()
    swaps[1].wait_recv()
    a2a_all.wait_recv()

    spread[...] = by_head[...].reshape(1024, 128).astype(F32)
    for half in range(2):
        parts = []
        for row in range(ROWS_DEV):
            parts.append(
                jnp.concatenate(
                    [
                        spread[pl.ds(row * 8 + half * 4 + chunk, 64, stride=16), :].astype(BF16)
                        for chunk in range(4)
                    ],
                    axis=1,
                )
            )
        heads_buf[:, half * 128 : half * 128 + 128] = jnp.dot(
            jnp.concatenate(parts), vu_buf[half], preferred_element_type=F32
        ).astype(BF16)

    for kind in range(3):
        heads_by_axis[kind] = jnp.dot(
            to_axis[kind], heads_buf[...], preferred_element_type=F32
        ).astype(BF16)

    def axis_copy(chunk, source, target, phase, to):
        axis = axes[chunk]
        return pltpu.make_async_remote_copy(
            source,
            target,
            axis_send.at[phase, chunk],
            axis_recv.at[phase, chunk],
            device_id=(sec, axis.dev(to, places[chunk][1])),
            device_id_type=MESH,
        )

    def axis_all(chunk, target, phase):
        whole = target[chunk].at[pl.ds(0, 3)]
        return axis_copy(chunk, whole, whole, phase, lax.rem(places[chunk][0] + 1, 4))

    def start_reduce(chunk, outgoing, incoming, phase):
        g, o = places[chunk]
        for step in (2, 1, 3):
            to = lax.rem(g + step, 4)
            axis_copy(
                chunk, outgoing[chunk].at[to], incoming[chunk].at[g], phase, to
            ).start()
        incoming[chunk][g] = outgoing[chunk][g]

    def plane_copy(chunk, source, target, phase, to):
        return pltpu.make_async_remote_copy(
            source,
            target,
            plane_send.at[phase, chunk],
            plane_recv.at[phase, chunk],
            device_id=(sec, axes[chunk].dev(places[chunk][0], to)),
            device_id_type=MESH,
        )

    def plane_all(chunk, target, phase):
        whole = target[chunk].at[pl.ds(0, 15)]
        return plane_copy(chunk, whole, whole, phase, lax.rem(places[chunk][1] + 1, 16))

    def start_plane(chunk, source_of, target, phase):
        g, o = places[chunk]

        for x, high, low in FAR_FIRST:
            if x == 0:
                to = (o // 4 + high) % 4 * 4 + (o + low) % 4
                plane_copy(chunk, source_of(to), target[chunk].at[o], phase, to).start()

    def reduce_axis(chunk, incoming, outgoing, target, phase):
        g, o = places[chunk]
        axis_all(chunk, incoming, phase).wait_recv()
        sub = SUBS[chunk]
        for tile in range(TILES[chunk]):
            columns = slice(tile * 128, tile * 128 + 128)
            total = incoming[chunk][0, :, columns].astype(F32)
            for slot in range(1, 4):
                total = total + incoming[chunk][slot, :, columns].astype(F32)
            for row in range(ROWS_DEV):
                lanes[chunk][pl.ds(row * sub + tile, 16, stride=2 * sub), :] = total[
                    row * 16 : row * 16 + 16
                ]
        outgoing[chunk][...] = lanes[chunk][...].reshape(16, 2 * sub, 128).astype(BF16)
        start_plane(chunk, lambda to: outgoing[chunk].at[to], target, phase)
        target[chunk][o] = outgoing[chunk][o]

    def reduce_plane(chunk, target, phase):
        plane_all(chunk, target, phase).wait_recv()
        return jnp.sum(target[chunk][...].astype(F32), axis=0)

    def send_sums(chunk):
        heads = heads_by_axis[axes[chunk].kind]
        columns = columns_of(chunk)
        product = jnp.dot(
            heads[:, 0:128], op_buf[0, :, columns], preferred_element_type=F32
        ) + jnp.dot(heads[:, 128:256], op_buf[1, :, columns], preferred_element_type=F32)
        sums_out[chunk][...] = product.astype(BF16).reshape(sums_out[chunk].shape)
        start_reduce(chunk, sums_out, sums_in, 0)

    def add_sums(chunk):
        reduce_axis(chunk, sums_in, plane_out, plane_in, 0)

    square = [jnp.zeros((1, 1), F32) for row in range(ROWS_DEV)]

    def send_rows(chunk):
        resid = hidden_buf[chunk][...] + reduce_plane(chunk, plane_in, 0)
        resid_buf[chunk][...] = resid
        gather_out[chunk][...] = (resid * gain_buf[chunk][...]).astype(BF16)
        start_plane(chunk, lambda to: gather_out[chunk], gather_in, 1)
        gather_in[chunk][places[chunk][1]] = gather_out[chunk][...]
        for row in range(ROWS_DEV):
            piece = resid[row * SUBS[chunk] : row * SUBS[chunk] + SUBS[chunk]]
            square[row] = square[row] + jnp.sum(piece * piece, keepdims=True)

    def send_routes():
        lane = iota(1, (1, 128))
        tile_rows = iota(0, (16, 128))
        tile = jnp.zeros((16, 128), F32)
        for row in range(ROWS_DEV):
            dense = jnp.zeros((1, 128), F32)
            for slot in range(8):
                dense = dense + jnp.where(
                    lane % EXPERTS == ids_ref[row, slot], route_ref[row, slot], 0.0
                )
            factor = lax.rsqrt(square[row] / 7168.0 + 1e-06)
            dense = jnp.where(lane < 48, dense, jnp.broadcast_to(factor, (1, 128)))
            high, middle, low = three_terms(dense)
            line = jnp.where(
                (lane < 16) | (lane == 48),
                high,
                jnp.where(
                    (lane < 32) | (lane == 49),
                    middle,
                    jnp.where((lane < 48) | (lane == 50), low, 0.0),
                ),
            )
            tile = jnp.where(tile_rows == row * SUBS[CHUNKS], line, tile)
        gather_out[CHUNKS][...] = tile.astype(BF16)
        start_plane(CHUNKS, lambda to: gather_out[CHUNKS], gather_in, 1)
        gather_in[CHUNKS][places[CHUNKS][1]] = gather_out[CHUNKS][...]

    def spread_rows(chunk):
        g, o = places[chunk]
        plane_all(chunk, gather_in, 1).wait_recv()
        sub = SUBS[chunk]
        lanes[chunk][...] = gather_in[chunk][...].reshape(32 * sub, 128).astype(F32)
        for tile in range(TILES[chunk]):
            for row in range(ROWS_DEV):
                rows_in[chunk][
                    g, row * 16 : row * 16 + 16, tile * 128 : tile * 128 + 128
                ] = lanes[chunk][pl.ds(row * sub + tile, 16, stride=2 * sub), :].astype(BF16)
        for step in (2, 1, 3):
            axis_copy(
                chunk, rows_in[chunk].at[g], rows_in[chunk].at[g], 1, lax.rem(g + step, 4)
            ).start()

    gate = [jnp.zeros((128, 256), F32) for piece in range(2)]
    upper = [jnp.zeros((128, 256), F32) for piece in range(2)]

    def common_order(chunk, block):
        if axes[chunk].kind == 0:
            return block
        return jnp.dot(
            from_axis[axes[chunk].kind], block, preferred_element_type=F32
        ).astype(BF16)

    def expert_in(chunk):
        axis_all(chunk, rows_in, 1).wait_recv()
        block = common_order(chunk, rows_in[chunk][...].reshape(128, TILES[chunk] * 128))
        depth = columns_of(chunk)
        for piece in range(2):
            gate[piece] = gate[piece] + jnp.dot(
                block, wg_buf[piece, depth, :], preferred_element_type=F32
            )
            upper[piece] = upper[piece] + jnp.dot(
                block, wu_buf[piece, depth, :], preferred_element_type=F32
            )

    def each(step, wave):
        for chunk in WAVES[wave]:
            step(chunk)

    each(send_sums, 0)
    each(send_sums, 1)
    for swap in swaps[2:]:
        swap.start()
    each(add_sums, 0)
    each(add_sums, 1)
    each(send_rows, 0)
    each(send_rows, 1)
    send_routes()
    each(spread_rows, 0)
    each(spread_rows, 1)
    spread_rows(CHUNKS)
    for index in range(2, 5):
        loads[index].wait()
        swaps[index].wait_recv()
    each(expert_in, 0)
    each(expert_in, 1)

    axis_all(CHUNKS, rows_in, 1).wait_recv()
    named = common_order(CHUNKS, rows_in[CHUNKS][...].reshape(128, 128))
    factor = jnp.sum(
        jnp.where((cols_i >= 48) & (cols_i < 51), named.astype(F32), 0.0), axis=1, keepdims=True
    )
    rows_all[:, 512:640] = named
    for piece in range(2):
        value = factor * gate[piece]
        rows_all[:, piece * 256 : piece * 256 + 256] = (
            value / (1.0 + jnp.exp(-value)) * (factor * upper[piece])
        ).astype(BF16)
    for kind in range(3):
        hidden_units = jnp.dot(back_axis[kind], rows_all[...], preferred_element_type=F32)
        units_by_axis[kind] = hidden_units[:, 0:512].astype(BF16)
        for piece in range(2):
            expert = piece * 8 + me // 8
            mine = (cols_i < 48) & (cols_i % EXPERTS == expert)
            weight = jnp.sum(
                jnp.where(mine, hidden_units[:, 512:640], 0.0), axis=1, keepdims=True
            )
            weight_by_axis[kind, piece] = jnp.broadcast_to(weight, (128, 128))

    def send_back(chunk):
        units = units_by_axis[axes[chunk].kind]
        columns = columns_of(chunk)
        product = jnp.zeros((128, TILES[chunk] * 128), F32)
        for piece in range(2):
            weight = weight_by_axis[axes[chunk].kind, piece]
            product = product + jnp.concatenate([weight] * TILES[chunk], axis=1) * jnp.dot(
                units[:, piece * 256 : piece * 256 + 256],
                wd_buf[piece, :, columns],
                preferred_element_type=F32,
            )
        back_out[chunk][...] = product.astype(BF16).reshape(back_out[chunk].shape)
        start_reduce(chunk, back_out, back_in, 2)

    def add_back(chunk):
        reduce_axis(chunk, back_in, plane_out2, plane_in2, 2)

    def finish(chunk):
        total = resid_buf[chunk][...] + reduce_plane(chunk, plane_in2, 2)
        for tile in range(TILES[chunk]):
            column = (FIRST[chunk] + tile) * 128
            for row in range(ROWS_DEV):
                at = row * SUBS[chunk] + tile
                out_ref[row : row + 1, column : column + 128] = total[at : at + 1, :]

    each(send_back, 0)
    each(send_back, 1)
    each(add_back, 0)
    each(add_back, 1)
    each(finish, 0)
    each(finish, 1)

    for swap in swaps:
        swap.wait_send()
    a2a_all.wait_send()
    for chunk in range(CHUNKS):
        axis_all(chunk, sums_in, 0).wait_send()
        axis_all(chunk, rows_in, 1).wait_send()
        axis_all(chunk, back_in, 2).wait_send()
        for phase, target in enumerate((plane_in, gather_in, plane_in2)):
            plane_all(chunk, target, phase).wait_send()
    axis_all(CHUNKS, rows_in, 1).wait_send()
    plane_all(CHUNKS, gather_in, 1).wait_send()


def layer(lengths, queries, cache, hidden_in, expert_ids, route_weights, norm_gain, value_up, out_proj, w_gate, w_up, w_down):
    vmem = pl.BlockSpec(memory_space=pltpu.VMEM)
    hbm = pl.BlockSpec(memory_space=pl.ANY)
    dma = pltpu.SemaphoreType.DMA
    wides = [tiles * 128 for tiles in TILES]
    return pl.pallas_call(
        layer_kernel,
        out_shape=jax.ShapeDtypeStruct((2, 7168), F32),
        in_specs=[hbm, hbm, hbm, hbm, hbm, hbm, hbm, hbm, hbm, hbm, hbm, hbm],
        out_specs=vmem,
        scratch_shapes=[
            pltpu.SMEM((2,), jnp.int32),
            pltpu.SMEM((2, 8), jnp.int32),
            pltpu.SMEM((2, 8), F32),
            pltpu.VMEM((2, 576, 128), BF16),
            pltpu.VMEM((2, 7168), BF16),
            pltpu.VMEM((1, 7168), F32),
            pltpu.VMEM((2, 576, 2048), BF16),
            pltpu.VMEM((2, 128, 2048), F32),
            pltpu.VMEM((2, 128, 2048), BF16),
            pltpu.VMEM((2, 512, 128), BF16),
            pltpu.VMEM((2, 128, 7168), BF16),
            pltpu.VMEM((2, 7168, 256), BF16),
            pltpu.VMEM((2, 7168, 256), BF16),
            pltpu.VMEM((2, 256, 7168), BF16),
            pltpu.VMEM((64, 16, 128), BF16),
            pltpu.VMEM((64, 16, 128), BF16),
            pltpu.VMEM((1024, 128), F32),
            pltpu.VMEM((128, 256), BF16),
            [pltpu.VMEM((4, 32, wide), BF16) for wide in wides],
            [pltpu.VMEM((4, 32, wide), BF16) for wide in wides],
            [pltpu.VMEM((32 * sub, 128), F32) for sub in SUBS],
            [pltpu.VMEM((16, 2 * sub, 128), BF16) for sub in SUBS],
            [pltpu.VMEM((16, 2 * sub, 128), BF16) for sub in SUBS],
            [pltpu.VMEM((2 * sub, 128), F32) for sub in SUBS],
            [pltpu.VMEM((2 * sub, 128), F32) for sub in SUBS],
            [pltpu.VMEM((2 * sub, 128), F32) for sub in SUBS],
            [pltpu.VMEM((16, 2 * sub, 128), BF16) for sub in SUBS],
            [pltpu.VMEM((2 * sub, 128), BF16) for sub in SUBS],
            [pltpu.VMEM((4, 32, wide), BF16) for wide in wides],
            pltpu.VMEM((128, 640), BF16),
            pltpu.VMEM((3, 128, 128), BF16),
            pltpu.VMEM((3, 128, 128), BF16),
            pltpu.VMEM((3, 128, 128), BF16),
            pltpu.VMEM((3, 128, 256), BF16),
            pltpu.VMEM((3, 128, 512), BF16),
            pltpu.VMEM((3, 2, 128, 128), F32),
            [pltpu.VMEM((4, 32, wide), BF16) for wide in wides],
            [pltpu.VMEM((4, 32, wide), BF16) for wide in wides],
            [pltpu.VMEM((16, 2 * sub, 128), BF16) for sub in SUBS],
            [pltpu.VMEM((16, 2 * sub, 128), BF16) for sub in SUBS],
            dma((6,)),
            dma((2, 4)),
            dma((5,)),
            dma((5,)),
            dma((5,)),
            dma,
            dma,
            dma((3, CHUNKS + 1)),
            dma((3, CHUNKS + 1)),
            dma((3, CHUNKS + 1)),
            dma((3, CHUNKS + 1)),
        ],
        compiler_params=pltpu.CompilerParams(
            collective_id=0, has_side_effects=True, vmem_limit_bytes=58 * MIB
        ),
        name="layer",
    )(
        lengths,
        queries,
        cache,
        hidden_in,
        expert_ids,
        route_weights,
        norm_gain.reshape(1, -1),
        value_up.reshape(512, 128),
        out_proj,
        w_gate,
        w_up,
        w_down,
    )


def per_device(
    hidden_in,
    queries,
    latent_cache,
    cache_lengths,
    value_up,
    out_proj,
    norm_gain,
    expert_ids,
    route_weights,
    w_gate,
    w_up,
    w_down,
):
    out = layer(
        cache_lengths,
        queries.transpose(0, 2, 1),
        latent_cache.transpose(0, 2, 1),
        hidden_in,
        expert_ids,
        route_weights,
        norm_gain,
        value_up,
        out_proj,
        w_gate,
        w_up,
        w_down,
    )
    return out.astype(BF16)


def solution(mesh):
    rows = P(("sec", "dev"), None)
    rows3 = P(("sec", "dev"), None, None)
    placed = (
        rows,
        rows3,
        rows3,
        P(("sec", "dev")),
        rows3,
        rows,
        P(),
        rows,
        rows,
        P(None, ("sec", "dev")),
        P(None, ("sec", "dev")),
        rows,
    )
    return jax.shard_map(
        per_device, mesh=mesh, in_specs=placed, out_specs=rows, check_vma=False
    )
```

```python
import jax
import jax.numpy as jnp
from jax import lax
from jax.experimental import pallas as pl
from jax.experimental.pallas import tpu as pltpu
from jax.sharding import PartitionSpec as P

EXPERTS = 16
ROWS_DEV = 2
MESH = pl.DeviceIdType.MESH
F32 = jnp.float32
BF16 = jnp.bfloat16
MIB = 2**20

score_scale = 0.07216878364870322

TILES = (11, 11, 10, 8, 8, 8, 1)
SUBS = (16, 16, 16, 8, 8, 8, 8)
FIRST = (0, 11, 22, 32, 40, 48)
CHUNKS = 6
WAVES = ((0, 1, 2), (3, 4, 5))
RING = (0, 1, 2, 1)
FAR_FIRST = sorted(
    [(x, z, y) for x in range(4) for z in range(4) for y in range(4)][1:],
    key=lambda at: -RING[at[0]] - RING[at[1]] - RING[at[2]],
)


def columns_of(chunk):
    return slice(FIRST[chunk] * 128, (FIRST[chunk] + TILES[chunk]) * 128)


class Axis:
    def __init__(self, kind):
        self.kind = kind
        self.first = (16, 4, 1)[kind]
        self.high = (4, 16, 16)[kind]
        self.low = (1, 1, 4)[kind]

    def dev(self, g, o):
        return g * self.first + (o // 4) * self.high + (o % 4) * self.low

    def place(self, dev):
        return (dev // self.first) % 4, (dev // self.high) % 4 * 4 + (dev // self.low) % 4

    def key(self, q):
        return ((q // 16) % 2) * 64 + self.dev(q // 32, q % 16)


def one_hot(rows_key, cols_key):
    return jnp.where(rows_key == cols_key, 1.0, 0.0).astype(BF16)


def iota(axis, shape=(128, 128)):
    return lax.broadcasted_iota(jnp.int32, shape, axis)


def three_terms(value):
    high = value.astype(BF16).astype(F32)
    middle = (value - high).astype(BF16).astype(F32)
    return high, middle, value - high - middle


def layer_kernel(
    lengths_hbm,
    queries_ref,
    cache_ref,
    hidden_ref,
    ids_hbm,
    route_hbm,
    gain_ref,
    value_up_ref,
    out_proj_ref,
    w_gate_ref,
    w_up_ref,
    w_down_ref,
    out_ref,
    lengths_ref,
    ids_ref,
    route_ref,
    query_buf,
    hidden_rows,
    gain_row,
    cache_buf,
    score_buf,
    weight_buf,
    vu_buf,
    op_buf,
    wg_buf,
    wu_buf,
    wd_buf,
    msg_buf,
    by_head,
    spread,
    heads_buf,
    sums_out,
    sums_in,
    lanes,
    plane_out,
    plane_in,
    resid_buf,
    hidden_buf,
    gain_buf,
    gather_in,
    gather_out,
    rows_in,
    rows_all,
    to_axis,
    from_axis,
    back_axis,
    heads_by_axis,
    units_by_axis,
    back_out,
    back_in,
    plane_out2,
    plane_in2,
    small_sem,
    cache_sem,
    load_sem,
    swap_send,
    swap_recv,
    a2a_send,
    a2a_recv,
    axis_send,
    axis_recv,
    plane_send,
    plane_recv,
):
    sec = lax.axis_index("sec")
    me = lax.axis_index("dev")
    axes = [Axis(kind) for kind in (0, 1, 2, 0, 1, 2, 2)]
    places = [axis.place(me) for axis in axes]

    barrier = pltpu.get_barrier_semaphore()

    def greet_all():
        for step in range(1, 64):
            pl.semaphore_signal(
                barrier, inc=1, device_id=(sec, lax.rem(me + step, 64)), device_id_type=MESH
            )
        pl.semaphore_signal(barrier, inc=1, device_id=(1 - sec, me), device_id_type=MESH)

    weights = (
        (value_up_ref, vu_buf),
        (out_proj_ref, op_buf),
        (w_gate_ref, wg_buf),
        (w_up_ref, wu_buf),
        (w_down_ref, wd_buf),
    )
    loads = [
        pltpu.make_async_copy(source, target.at[sec], load_sem.at[index])
        for index, (source, target) in enumerate(weights)
    ]
    swaps = [
        pltpu.make_async_remote_copy(
            source,
            target.at[sec],
            swap_send.at[index],
            swap_recv.at[index],
            device_id=(1 - sec, me),
            device_id_type=MESH,
        )
        for index, (source, target) in enumerate(weights)
    ]
    cache_loads = []
    for row in range(ROWS_DEV):
        for piece in range(4):
            depth = pl.ds(piece * 144, 144)
            cache_loads.append(
                pltpu.make_async_copy(
                    cache_ref.at[row, depth, :],
                    cache_buf.at[row, depth, :],
                    cache_sem.at[row, piece],
                )
            )
    small_loads = [
        pltpu.make_async_copy(source, target, small_sem.at[index])
        for index, (source, target) in enumerate(
            (
                (queries_ref, query_buf),
                (hidden_ref, hidden_rows),
                (gain_ref, gain_row),
                (lengths_hbm, lengths_ref),
                (ids_hbm, ids_ref),
                (route_hbm, route_ref),
            )
        )
    ]
    for copy in [small_loads[0]] + cache_loads + small_loads[1:]:
        copy.start()
    greet_all()
    small_loads[0].wait()
    small_loads[3].wait()
    for load in cache_loads:
        load.wait()
    for load in loads[:2]:
        load.start()

    span, step_len = cache_ref.shape[2], 512
    for row in range(ROWS_DEV):
        length = lengths_ref[row]
        query = query_buf[row].T
        peak = jnp.full((128, 1), -1e30, F32)
        for start in range(0, span, step_len):
            score = jnp.dot(
                query, cache_buf[row, :, start : start + step_len], preferred_element_type=F32
            )
            position = start + iota(1, (1, step_len))
            score = jnp.where(position < length, score * score_scale, -1e30)
            score_buf[row, :, start : start + step_len] = score
            peak = jnp.maximum(peak, jnp.max(score, axis=1, keepdims=True))
        total = jnp.zeros((128, 1), F32)
        for start in range(0, span, step_len):
            weight = jnp.exp(score_buf[row, :, start : start + step_len] - peak)
            total = total + jnp.sum(weight, axis=1, keepdims=True)
            weight_buf[row, :, start : start + step_len] = weight.astype(BF16)
        summed = lax.dot_general(
            cache_buf[row, 0:512, :],
            weight_buf[row],
            (((1,), (1,)), ((), ())),
            preferred_element_type=F32,
        )
        attended = summed.T / total
        for half in range(2):
            for chunk in range(4):
                spread[pl.ds(row * 8 + half * 4 + chunk, 64, stride=16), :] = attended[
                    half * 64 : half * 64 + 64, chunk * 128 : chunk * 128 + 128
                ]
    pl.semaphore_wait(barrier, 64)
    swaps[0].start()
    swaps[1].start()
    msg_buf[...] = spread[...].astype(BF16).reshape(64, 16, 128)

    for x, z, y in FAR_FIRST:
        peer = (me // 16 + x) % 4 * 16 + (me // 4 % 4 + z) % 4 * 4 + (me + y) % 4
        pltpu.make_async_remote_copy(
            msg_buf.at[peer],
            by_head.at[me],
            a2a_send,
            a2a_recv,
            device_id=(sec, peer),
            device_id_type=MESH,
        ).start()
    by_head[me] = msg_buf[me]

    rows_i, cols_i = iota(0), iota(1)
    for kind in range(3):
        to_axis[kind] = one_hot(Axis(kind).key(rows_i), cols_i)
        from_axis[kind] = one_hot(Axis(0).key(rows_i), Axis(kind).key(cols_i))
        back_axis[kind] = one_hot(Axis(kind).key(rows_i), Axis(0).key(cols_i))
    for index in (1, 4, 5):
        small_loads[index].wait()
    small_loads[2].wait()
    hidden = hidden_rows[...].astype(F32)
    gains = gain_row[...]
    for chunk in range(CHUNKS):
        hidden_buf[chunk][...] = jnp.zeros(hidden_buf[chunk].shape, F32)
        gain_buf[chunk][...] = jnp.zeros(gain_buf[chunk].shape, F32)
        lanes[chunk][...] = jnp.zeros(lanes[chunk].shape, F32)
        for tile in range(TILES[chunk]):
            column = (FIRST[chunk] + tile) * 128
            for row in range(ROWS_DEV):
                at = row * SUBS[chunk] + tile
                hidden_buf[chunk][at : at + 1, :] = hidden[row : row + 1, column : column + 128]
                gain_buf[chunk][at : at + 1, :] = gains[:, column : column + 128]

    a2a_all = pltpu.make_async_remote_copy(
        msg_buf.at[pl.ds(0, 63)],
        by_head.at[pl.ds(0, 63)],
        a2a_send,
        a2a_recv,
        device_id=(sec, lax.rem(me + 1, 64)),
        device_id_type=MESH,
    )
    loads[0].wait()
    loads[1].wait()
    swaps[0].wait_recv()
    swaps[1].wait_recv()
    a2a_all.wait_recv()

    spread[...] = by_head[...].reshape(1024, 128).astype(F32)
    for half in range(2):
        parts = []
        for row in range(ROWS_DEV):
            parts.append(
                jnp.concatenate(
                    [
                        spread[pl.ds(row * 8 + half * 4 + chunk, 64, stride=16), :].astype(BF16)
                        for chunk in range(4)
                    ],
                    axis=1,
                )
            )
        heads_buf[:, half * 128 : half * 128 + 128] = jnp.dot(
            jnp.concatenate(parts), vu_buf[half], preferred_element_type=F32
        ).astype(BF16)

    for kind in range(3):
        heads_by_axis[kind] = jnp.dot(
            to_axis[kind], heads_buf[...], preferred_element_type=F32
        ).astype(BF16)

    def axis_copy(chunk, source, target, phase, to):
        axis = axes[chunk]
        return pltpu.make_async_remote_copy(
            source,
            target,
            axis_send.at[phase, chunk],
            axis_recv.at[phase, chunk],
            device_id=(sec, axis.dev(to, places[chunk][1])),
            device_id_type=MESH,
        )

    def axis_all(chunk, target, phase):
        whole = target[chunk].at[pl.ds(0, 3)]
        return axis_copy(chunk, whole, whole, phase, lax.rem(places[chunk][0] + 1, 4))

    def start_reduce(chunk, outgoing, incoming, phase):
        g, o = places[chunk]
        for step in (2, 1, 3):
            to = lax.rem(g + step, 4)
            axis_copy(
                chunk, outgoing[chunk].at[to], incoming[chunk].at[g], phase, to
            ).start()
        incoming[chunk][g] = outgoing[chunk][g]

    def plane_copy(chunk, source, target, phase, to):
        return pltpu.make_async_remote_copy(
            source,
            target,
            plane_send.at[phase, chunk],
            plane_recv.at[phase, chunk],
            device_id=(sec, axes[chunk].dev(places[chunk][0], to)),
            device_id_type=MESH,
        )

    def plane_all(chunk, target, phase):
        whole = target[chunk].at[pl.ds(0, 15)]
        return plane_copy(chunk, whole, whole, phase, lax.rem(places[chunk][1] + 1, 16))

    def start_plane(chunk, source_of, target, phase):
        g, o = places[chunk]

        for x, high, low in FAR_FIRST:
            if x == 0:
                to = (o // 4 + high) % 4 * 4 + (o + low) % 4
                plane_copy(chunk, source_of(to), target[chunk].at[o], phase, to).start()

    def reduce_axis(chunk, incoming, outgoing, target, phase):
        g, o = places[chunk]
        axis_all(chunk, incoming, phase).wait_recv()
        sub = SUBS[chunk]
        for tile in range(TILES[chunk]):
            columns = slice(tile * 128, tile * 128 + 128)
            total = incoming[chunk][0, :, columns].astype(F32)
            for slot in range(1, 4):
                total = total + incoming[chunk][slot, :, columns].astype(F32)
            for row in range(ROWS_DEV):
                lanes[chunk][pl.ds(row * sub + tile, 16, stride=2 * sub), :] = total[
                    row * 16 : row * 16 + 16
                ]
        outgoing[chunk][...] = lanes[chunk][...].reshape(16, 2 * sub, 128).astype(BF16)
        start_plane(chunk, lambda to: outgoing[chunk].at[to], target, phase)
        target[chunk][o] = outgoing[chunk][o]

    def reduce_plane(chunk, target, phase):
        plane_all(chunk, target, phase).wait_recv()
        return jnp.sum(target[chunk][...].astype(F32), axis=0)

    def send_sums(chunk):
        heads = heads_by_axis[axes[chunk].kind]
        columns = columns_of(chunk)
        product = jnp.dot(
            heads,
            op_buf[:, :, columns].reshape(256, TILES[chunk] * 128),
            preferred_element_type=F32,
        )
        sums_out[chunk][...] = product.astype(BF16).reshape(sums_out[chunk].shape)
        start_reduce(chunk, sums_out, sums_in, 0)

    def add_sums(chunk):
        reduce_axis(chunk, sums_in, plane_out, plane_in, 0)

    square = [jnp.zeros((1, 1), F32) for row in range(ROWS_DEV)]

    def send_rows(chunk):
        resid = hidden_buf[chunk][...] + reduce_plane(chunk, plane_in, 0)
        resid_buf[chunk][...] = resid
        gather_out[chunk][...] = (resid * gain_buf[chunk][...]).astype(BF16)
        start_plane(chunk, lambda to: gather_out[chunk], gather_in, 1)
        gather_in[chunk][places[chunk][1]] = gather_out[chunk][...]
        for row in range(ROWS_DEV):
            piece = resid[row * SUBS[chunk] : row * SUBS[chunk] + SUBS[chunk]]
            square[row] = square[row] + jnp.sum(piece * piece, keepdims=True)

    def send_routes():
        lane = iota(1, (1, 128))
        tile_rows = iota(0, (16, 128))
        tile = jnp.zeros((16, 128), F32)
        for row in range(ROWS_DEV):
            dense = jnp.zeros((1, 128), F32)
            for slot in range(8):
                dense = dense + jnp.where(
                    lane % EXPERTS == ids_ref[row, slot], route_ref[row, slot], 0.0
                )
            factor = lax.rsqrt(square[row] / 7168.0 + 1e-06)
            dense = jnp.where(lane < 48, dense, jnp.broadcast_to(factor, (1, 128)))
            high, middle, low = three_terms(dense)
            line = jnp.where(
                (lane < 16) | (lane == 48),
                high,
                jnp.where(
                    (lane < 32) | (lane == 49),
                    middle,
                    jnp.where((lane < 48) | (lane == 50), low, 0.0),
                ),
            )
            tile = jnp.where(tile_rows == row * SUBS[CHUNKS], line, tile)
        gather_out[CHUNKS][...] = tile.astype(BF16)
        start_plane(CHUNKS, lambda to: gather_out[CHUNKS], gather_in, 1)
        gather_in[CHUNKS][places[CHUNKS][1]] = gather_out[CHUNKS][...]

    def spread_rows(chunk):
        g, o = places[chunk]
        plane_all(chunk, gather_in, 1).wait_recv()
        sub = SUBS[chunk]
        lanes[chunk][...] = gather_in[chunk][...].reshape(32 * sub, 128).astype(F32)
        for tile in range(TILES[chunk]):
            for row in range(ROWS_DEV):
                rows_in[chunk][
                    g, row * 16 : row * 16 + 16, tile * 128 : tile * 128 + 128
                ] = lanes[chunk][pl.ds(row * sub + tile, 16, stride=2 * sub), :].astype(BF16)
        for step in (2, 1, 3):
            axis_copy(
                chunk, rows_in[chunk].at[g], rows_in[chunk].at[g], 1, lax.rem(g + step, 4)
            ).start()

    gate = [jnp.zeros((128, 256), F32) for piece in range(2)]
    upper = [jnp.zeros((128, 256), F32) for piece in range(2)]

    def common_order(chunk, block):
        if axes[chunk].kind == 0:
            return block
        return jnp.dot(
            from_axis[axes[chunk].kind], block, preferred_element_type=F32
        ).astype(BF16)

    def expert_in(chunk):
        axis_all(chunk, rows_in, 1).wait_recv()
        block = common_order(chunk, rows_in[chunk][...].reshape(128, TILES[chunk] * 128))
        depth = columns_of(chunk)
        for piece in range(2):
            gate[piece] = gate[piece] + jnp.dot(
                block, wg_buf[piece, depth, :], preferred_element_type=F32
            )
            upper[piece] = upper[piece] + jnp.dot(
                block, wu_buf[piece, depth, :], preferred_element_type=F32
            )

    def each(step, wave):
        for chunk in WAVES[wave]:
            step(chunk)

    each(send_sums, 0)
    each(send_sums, 1)
    for copy in loads[2:] + swaps[2:]:
        copy.start()
    each(add_sums, 0)
    each(add_sums, 1)
    each(send_rows, 0)
    each(send_rows, 1)
    send_routes()
    each(spread_rows, 0)
    each(spread_rows, 1)
    spread_rows(CHUNKS)
    for index in range(2, 5):
        loads[index].wait()
        swaps[index].wait_recv()
    each(expert_in, 0)
    each(expert_in, 1)

    axis_all(CHUNKS, rows_in, 1).wait_recv()
    named = common_order(CHUNKS, rows_in[CHUNKS][...].reshape(128, 128))
    factor = jnp.sum(
        jnp.where((cols_i >= 48) & (cols_i < 51), named.astype(F32), 0.0), axis=1, keepdims=True
    )
    for piece in range(2):
        expert = piece * 8 + me // 8
        mine = (cols_i < 48) & (cols_i % EXPERTS == expert)
        weight = jnp.sum(jnp.where(mine, named.astype(F32), 0.0), axis=1, keepdims=True)
        value = factor * gate[piece]
        rows_all[:, piece * 256 : piece * 256 + 256] = (
            value / (1.0 + jnp.exp(-value)) * (factor * upper[piece]) * weight
        ).astype(BF16)
    units_by_axis[0] = rows_all[...]
    for kind in range(1, 3):
        units_by_axis[kind] = jnp.dot(
            back_axis[kind], rows_all[...], preferred_element_type=F32
        ).astype(BF16)

    def send_back(chunk):
        columns = columns_of(chunk)
        product = jnp.dot(
            units_by_axis[axes[chunk].kind],
            wd_buf[:, :, columns].reshape(512, TILES[chunk] * 128),
            preferred_element_type=F32,
        )
        back_out[chunk][...] = product.astype(BF16).reshape(back_out[chunk].shape)
        start_reduce(chunk, back_out, back_in, 2)

    def add_back(chunk):
        reduce_axis(chunk, back_in, plane_out2, plane_in2, 2)

    def finish(chunk):
        total = resid_buf[chunk][...] + reduce_plane(chunk, plane_in2, 2)
        for tile in range(TILES[chunk]):
            column = (FIRST[chunk] + tile) * 128
            for row in range(ROWS_DEV):
                at = row * SUBS[chunk] + tile
                out_ref[row : row + 1, column : column + 128] = total[at : at + 1, :]

    each(send_back, 0)
    each(send_back, 1)
    each(add_back, 0)
    each(add_back, 1)
    each(finish, 0)
    each(finish, 1)

    for swap in swaps:
        swap.wait_send()
    a2a_all.wait_send()
    for chunk in range(CHUNKS):
        axis_all(chunk, sums_in, 0).wait_send()
        axis_all(chunk, rows_in, 1).wait_send()
        axis_all(chunk, back_in, 2).wait_send()
        for phase, target in enumerate((plane_in, gather_in, plane_in2)):
            plane_all(chunk, target, phase).wait_send()
    axis_all(CHUNKS, rows_in, 1).wait_send()
    plane_all(CHUNKS, gather_in, 1).wait_send()


def layer(lengths, queries, cache, hidden_in, expert_ids, route_weights, norm_gain, value_up, out_proj, w_gate, w_up, w_down):
    vmem = pl.BlockSpec(memory_space=pltpu.VMEM)
    hbm = pl.BlockSpec(memory_space=pl.ANY)
    dma = pltpu.SemaphoreType.DMA
    wides = [tiles * 128 for tiles in TILES]
    return pl.pallas_call(
        layer_kernel,
        out_shape=jax.ShapeDtypeStruct((2, 7168), F32),
        in_specs=[hbm, hbm, hbm, hbm, hbm, hbm, hbm, hbm, hbm, hbm, hbm, hbm],
        out_specs=vmem,
        scratch_shapes=[
            pltpu.SMEM((2,), jnp.int32),
            pltpu.SMEM((2, 8), jnp.int32),
            pltpu.SMEM((2, 8), F32),
            pltpu.VMEM((2, 576, 128), BF16),
            pltpu.VMEM((2, 7168), BF16),
            pltpu.VMEM((1, 7168), F32),
            pltpu.VMEM((2, 576, 2048), BF16),
            pltpu.VMEM((2, 128, 2048), F32),
            pltpu.VMEM((2, 128, 2048), BF16),
            pltpu.VMEM((2, 512, 128), BF16),
            pltpu.VMEM((2, 128, 7168), BF16),
            pltpu.VMEM((2, 7168, 256), BF16),
            pltpu.VMEM((2, 7168, 256), BF16),
            pltpu.VMEM((2, 256, 7168), BF16),
            pltpu.VMEM((64, 16, 128), BF16),
            pltpu.VMEM((64, 16, 128), BF16),
            pltpu.VMEM((1024, 128), F32),
            pltpu.VMEM((128, 256), BF16),
            [pltpu.VMEM((4, 32, wide), BF16) for wide in wides],
            [pltpu.VMEM((4, 32, wide), BF16) for wide in wides],
            [pltpu.VMEM((32 * sub, 128), F32) for sub in SUBS],
            [pltpu.VMEM((16, 2 * sub, 128), BF16) for sub in SUBS],
            [pltpu.VMEM((16, 2 * sub, 128), BF16) for sub in SUBS],
            [pltpu.VMEM((2 * sub, 128), F32) for sub in SUBS],
            [pltpu.VMEM((2 * sub, 128), F32) for sub in SUBS],
            [pltpu.VMEM((2 * sub, 128), F32) for sub in SUBS],
            [pltpu.VMEM((16, 2 * sub, 128), BF16) for sub in SUBS],
            [pltpu.VMEM((2 * sub, 128), BF16) for sub in SUBS],
            [pltpu.VMEM((4, 32, wide), BF16) for wide in wides],
            pltpu.VMEM((128, 512), BF16),
            pltpu.VMEM((3, 128, 128), BF16),
            pltpu.VMEM((3, 128, 128), BF16),
            pltpu.VMEM((3, 128, 128), BF16),
            pltpu.VMEM((3, 128, 256), BF16),
            pltpu.VMEM((3, 128, 512), BF16),
            [pltpu.VMEM((4, 32, wide), BF16) for wide in wides],
            [pltpu.VMEM((4, 32, wide), BF16) for wide in wides],
            [pltpu.VMEM((16, 2 * sub, 128), BF16) for sub in SUBS],
            [pltpu.VMEM((16, 2 * sub, 128), BF16) for sub in SUBS],
            dma((6,)),
            dma((2, 4)),
            dma((5,)),
            dma((5,)),
            dma((5,)),
            dma,
            dma,
            dma((3, CHUNKS + 1)),
            dma((3, CHUNKS + 1)),
            dma((3, CHUNKS + 1)),
            dma((3, CHUNKS + 1)),
        ],
        compiler_params=pltpu.CompilerParams(
            collective_id=0, has_side_effects=True, vmem_limit_bytes=58 * MIB
        ),
        name="layer",
    )(
        lengths,
        queries,
        cache,
        hidden_in,
        expert_ids,
        route_weights,
        norm_gain.reshape(1, -1),
        value_up.reshape(512, 128),
        out_proj,
        w_gate,
        w_up,
        w_down,
    )


def per_device(
    hidden_in,
    queries,
    latent_cache,
    cache_lengths,
    value_up,
    out_proj,
    norm_gain,
    expert_ids,
    route_weights,
    w_gate,
    w_up,
    w_down,
):
    out = layer(
        cache_lengths,
        queries.transpose(0, 2, 1),
        latent_cache.transpose(0, 2, 1),
        hidden_in,
        expert_ids,
        route_weights,
        norm_gain,
        value_up,
        out_proj,
        w_gate,
        w_up,
        w_down,
    )
    return out.astype(BF16)


def solution(mesh):
    rows = P(("sec", "dev"), None)
    rows3 = P(("sec", "dev"), None, None)
    placed = (
        rows,
        rows3,
        rows3,
        P(("sec", "dev")),
        rows3,
        rows,
        P(),
        rows,
        rows,
        P(None, ("sec", "dev")),
        P(None, ("sec", "dev")),
        rows,
    )
    return jax.shard_map(
        per_device, mesh=mesh, in_specs=placed, out_specs=rows, check_vma=False
    )
```
